32 devices in a mesh: gz: 16 (over z, x, core), gy: 2 (over y).
Axes of the slice: x: 2, y: 2, z: 4, core: 2. Of those that a mesh axis runs over, the one named last changes fastest.
Arguments:
- saved_order_parameter: float32 [128, 32, 512], P('gz', 'gy'), may hold values from 0 to 1
- saved_heat_level: float32 [128, 32, 512], P('gz', 'gy'), may hold values from 0 to 1.5
- kinetic_rate_field: float32 [128, 32, 512], P('gz', 'gy'), may hold values from 0.5 to 2
- order_parameter_adjoint_seed: float32 [128, 32, 512], P('gz', 'gy'), may hold values from -6 to 6
- heat_level_adjoint_seed: float32 [128, 32, 512], P('gz', 'gy'), may hold values from -6 to 6
Outputs:
- start_phase: float32 [128, 32, 512], P('gz', 'gy')
- start_temp: float32 [128, 32, 512], P('gz', 'gy')
- grad_mobility: float32 [128, 32, 512], P('gz', 'gy')
The draws below stay inside these ranges and needn't reach their ends.
All inputs are finite; a program needn't handle non-finite values.
Results may differ from the reference program's by a relative error of at most 0.00002.
Values sent between devices are 32-bit elements; how exact they have to be, the bound alone decides.
A program may use at most 64 MiB of HBM per device.

```python
import math
import jax
import jax.numpy as jnp

GRID_LENGTH_EAST = 512
GRID_LENGTH_UPWARD = 128
GRID_LENGTH_NORTH = 32


def level_of(stream_key, extent, pieces, smallest, top_value):
    loudness, own = 1.0, jax.random.fold_in(stream_key, 6)
    for position, shards_of in pieces:
        heights = jnp.exp(jax.random.uniform(jax.random.fold_in(own, position), (shards_of,), jnp.float32, smallest / len(pieces), top_value / len(pieces)))
        loudness = loudness * jnp.repeat(heights, extent[position] // shards_of).reshape([-1 if axis == position else 1 for axis in range(len(extent))])
    return loudness


def scatter_about(rng, extent, width, bound, pieces=(), kind=jnp.bfloat16):
    drawn = width * jax.random.normal(rng, extent, jnp.float32)
    if pieces:
        drawn = drawn * level_of(rng, extent, pieces, -0.22, 0.18)
    return jnp.clip(drawn, -bound, bound).astype(kind)


def setup_inputs(seed: int = 0) -> dict:
    arg_keys = jax.random.split(jax.random.key(seed), 6)
    saved_order_parameter = jnp.clip(1.0 * jax.random.uniform(arg_keys[0], (GRID_LENGTH_UPWARD, GRID_LENGTH_NORTH, GRID_LENGTH_EAST), jnp.float32) ** level_of(arg_keys[0], (GRID_LENGTH_UPWARD, GRID_LENGTH_NORTH, GRID_LENGTH_EAST), ((0, 16), (1, 2)), -0.2, 0.2), 0.0, 1.0)
    saved_heat_level = jnp.clip(1.5 * jax.random.uniform(arg_keys[1], (GRID_LENGTH_UPWARD, GRID_LENGTH_NORTH, GRID_LENGTH_EAST), jnp.float32) ** level_of(arg_keys[1], (GRID_LENGTH_UPWARD, GRID_LENGTH_NORTH, GRID_LENGTH_EAST), ((0, 16), (1, 2)), -0.2, 0.2), 0.0, 1.5)
    kinetic_rate_field = jnp.clip(jnp.exp(math.log(2.0) - 1.3862944 * jax.random.uniform(arg_keys[2], (GRID_LENGTH_UPWARD, GRID_LENGTH_NORTH, GRID_LENGTH_EAST), jnp.float32) ** level_of(arg_keys[2], (GRID_LENGTH_UPWARD, GRID_LENGTH_NORTH, GRID_LENGTH_EAST), ((0, 16), (1, 2)), -0.2, 0.2)), 0.5, 2.0)
    order_parameter_adjoint_seed = scatter_about(arg_keys[3], (GRID_LENGTH_UPWARD, GRID_LENGTH_NORTH, GRID_LENGTH_EAST), 1.0, 6.0, ((0, 16), (1, 2)), jnp.float32)
    heat_level_adjoint_seed = scatter_about(arg_keys[4], (GRID_LENGTH_UPWARD, GRID_LENGTH_NORTH, GRID_LENGTH_EAST), 1.0, 6.0, ((0, 16), (1, 2)), jnp.float32)
    return {"saved_order_parameter": saved_order_parameter, "saved_heat_level": saved_heat_level, "kinetic_rate_field": kinetic_rate_field, "order_parameter_adjoint_seed": order_parameter_adjoint_seed, "heat_level_adjoint_seed": heat_level_adjoint_seed}


TIME_STEP = 0.15
ENERGY_SCALE = 0.5
ANISOTROPY = 0.05
GRAD_FLOOR = 0.01
LATENT_HEAT = 1.8
DRIVE_SCALE = 0.9
DRIVE_SHARP = 10.0
MELT_POINT = 1.0

def advance_solver_step(phase_wide, temp_wide, kinetic_rate_field):
    padded = jnp.pad(phase_wide, ((0, 0), (0, 0), (2, 2)))
    grad_z = 0.5 * (padded[2:, 1:-1, 1:-1] - padded[:-2, 1:-1, 1:-1])
    grad_y = 0.5 * (padded[1:-1, 2:, 1:-1] - padded[1:-1, :-2, 1:-1])
    grad_x = 0.5 * (padded[1:-1, 1:-1, 2:] - padded[1:-1, 1:-1, :-2])
    sq_z = grad_z * grad_z
    sq_y = grad_y * grad_y
    sq_x = grad_x * grad_x
    squared = sq_z + sq_y + sq_x + GRAD_FLOOR
    quartic = (sq_z * sq_z + sq_y * sq_y + sq_x * sq_x) / (squared * squared)
    anisotropy = 1.0 + ANISOTROPY * (4.0 * quartic - 3.0)
    aniso_sq = anisotropy * anisotropy
    factor_a = 16.0 * ANISOTROPY * anisotropy / squared
    flux_z = ENERGY_SCALE * (aniso_sq * grad_z + factor_a * grad_z * (sq_z - quartic * squared))
    flux_y = ENERGY_SCALE * (aniso_sq * grad_y + factor_a * grad_y * (sq_y - quartic * squared))
    flux_x = ENERGY_SCALE * (aniso_sq * grad_x + factor_a * grad_x * (sq_x - quartic * squared))
    divergence = 0.5 * (flux_z[2:, 1:-1, 1:-1] - flux_z[:-2, 1:-1, 1:-1])
    divergence = divergence + 0.5 * (flux_y[1:-1, 2:, 1:-1] - flux_y[1:-1, :-2, 1:-1])
    divergence = divergence + 0.5 * (flux_x[1:-1, 1:-1, 2:] - flux_x[1:-1, 1:-1, :-2])
    phase_now = phase_wide[2:-2, 2:-2]
    temp_now = temp_wide[2:-2, 2:-2]
    driving = DRIVE_SCALE / jnp.pi * jnp.arctan(DRIVE_SHARP * (MELT_POINT - temp_now))
    growth = kinetic_rate_field * (divergence + phase_now * (1.0 - phase_now) * (phase_now - 0.5 + driving))
    new_phase = phase_now + TIME_STEP * growth
    temp_x = jnp.pad(temp_now, ((0, 0), (0, 0), (1, 1)))
    laplacian = temp_wide[3:-1, 2:-2] + temp_wide[1:-3, 2:-2] + temp_wide[2:-2, 3:-1] + temp_wide[2:-2, 1:-3]
    laplacian = laplacian + temp_x[:, :, 2:] + temp_x[:, :, :-2] - 6.0 * temp_now
    new_temp = temp_now + TIME_STEP * laplacian + LATENT_HEAT * (new_phase - phase_now)
    return (new_phase, new_temp)

def widen_slices(field):
    return jnp.pad(field, ((2, 2), (2, 2), (0, 0)))

def advance_mapping(saved_order_parameter, saved_heat_level, kinetic_rate_field):
    return advance_solver_step(widen_slices(saved_order_parameter), widen_slices(saved_heat_level), kinetic_rate_field)

def reference(saved_order_parameter, saved_heat_level, kinetic_rate_field, order_parameter_adjoint_seed, heat_level_adjoint_seed):
    succeeding_order_parameter, succeeding_heat_level = advance_mapping(saved_order_parameter, saved_heat_level, kinetic_rate_field)
    discarded_result, sensitivity_latest = jax.vjp(advance_mapping, succeeding_order_parameter, succeeding_heat_level, kinetic_rate_field)
    halfway_order_parameter, halfway_heat_level, latest_kinetic_rate = sensitivity_latest((order_parameter_adjoint_seed, heat_level_adjoint_seed))
    discarded_result, prior_backward_sweep = jax.vjp(advance_mapping, saved_order_parameter, saved_heat_level, kinetic_rate_field)
    start_phase, start_temp, early_mob = prior_backward_sweep((halfway_order_parameter, halfway_heat_level))
    return (start_phase, start_temp, latest_kinetic_rate + early_mob)
```

```python
import functools
import math

import jax
import jax.numpy as jnp
from jax import lax
from jax.experimental import pallas as pl
from jax.experimental.pallas import tpu as pltpu
from jax.sharding import PartitionSpec as P

TIME_STEP = 0.15
ANISOTROPY = 0.05
GRAD_FLOOR = 0.01
LATENT_HEAT = 1.8
DRIVE_SCALE = 0.9
DRIVE_SHARP = 10.0
MELT_POINT = 1.0

BASE = 1.0 - 3.0 * ANISOTROPY
RISE = 4.0 * ANISOTROPY
HALF_BASE = 0.5 * BASE
FALL = 8.0 * ANISOTROPY - 0.5 * RISE
TWIST = 8.0 * ANISOTROPY
SLOPE_0 = RISE * HALF_BASE - FALL * BASE
SLOPE_1 = -2.0 * RISE * FALL
FLOOR = 4.0 * GRAD_FLOOR

ATAN = (
    1.0, -0.3333328366279602, 0.19998230040073395, -0.14261573553085327,
    0.10940198600292206, -0.08372063934803009, 0.05746355652809143,
    -0.030717508867383003, 0.010680719278752804, -0.0017437011701986194,
)

SIDES = ((1, 0), (-1, 0), (0, 1), (0, -1), (1, 1), (1, -1), (-1, 1), (-1, -1))
ROW = 8


def recip(x):
    r = pl.reciprocal(x, approx=True)
    return r * (2.0 - x * r)


def arctan(x):
    size = jnp.abs(x)
    big = size > 1.0
    y = jnp.where(big, recip(jnp.maximum(size, 1.0)), size)
    z = y * y
    total = jnp.full_like(z, ATAN[-1])
    for c in ATAN[-2::-1]:
        total = total * z + c
    total = total * y
    total = jnp.where(big, 0.5 * math.pi - total, total)
    return jnp.where(x < 0.0, -total, total)


def basis(dz, dy, dx):
    zz, yy, xx = dz * dz, dy * dy, dx * dx
    s = zz + yy + xx + FLOOR
    r = recip(s)
    qs = (zz * zz + yy * yy + xx * xx) * r
    q = qs * r
    a = BASE + RISE * q
    big_a = a * (HALF_BASE - FALL * q)
    big_b = TWIST * a * r
    return zz, yy, xx, r, qs, q, a, big_a, big_b


def flux_of(d, sq, b):
    return d * (b[7] + b[8] * sq)


def tangent(dz, dy, dx, ez, ey, ex, b):
    zz, yy, xx, r, qs, q, a, big_a, big_b = b
    mz, my, mx = dz * ez, dy * ey, dx * ex
    g = mz + my + mx
    t = zz * mz + yy * my + xx * mx
    dq = (4.0 * r * r) * (t - qs * g)
    d_a = (SLOPE_0 + SLOPE_1 * q) * dq
    d_b = r * (TWIST * RISE * dq - (2.0 * TWIST) * a * r * g)
    return big_a, 3.0 * big_b, d_a, d_b


def turn(d, sq, e, t):
    return (t[0] + t[1] * sq) * e + d * (t[2] + t[3] * sq)


def kernel(
    nz, ny,
    p_in, u_in, k_in, ps_in, ts_in,
    sp_out, st_out, gm_out,
    p0, p1, d1, d0, u0, t1, t0, u1,
    jz, jy, jx, gz, gy, gx,
    r0, rp0, ru0, r1, rp1, ru1, tl1, gr0, pb0,
    sy0, ry0, sy1, ry1, sy2, ry2, sy3, ry3,
    sc0, rc0, sc1, rc1, sc2, rc2,
    ssem, rsem,
):
    Z, Y, X = p_in.shape
    tiles = range(Y // 8)
    zi, yi = lax.axis_index("gz"), lax.axis_index("gy")

    def there(side):
        cond = None
        for step, at, count in ((side[0], zi, nz), (side[1], yi, ny)):
            if step:
                c = at < count - 1 if step > 0 else at > 0
                cond = c if cond is None else jnp.logical_and(cond, c)
        return cond

    def opposite(side):
        return (-side[0], -side[1])

    barrier = pltpu.get_barrier_semaphore()
    for side in SIDES:
        @pl.when(there(side))
        def _(side=side):
            pl.semaphore_signal(
                barrier, inc=1, device_id=(zi + side[0], yi + side[1]),
                device_id_type=pl.DeviceIdType.MESH,
            )

    slots = iter(range(1000))

    def message(side, src, dst):
        slot = next(slots)
        copy = pltpu.make_async_remote_copy(
            src_ref=src, dst_ref=dst, send_sem=ssem.at[slot], recv_sem=rsem.at[slot],
            device_id=(zi + side[0], yi + side[1]), device_id_type=pl.DeviceIdType.MESH,
        )
        return side, copy

    def start(messages):
        for side, copy in messages:
            pl.when(there(side))(copy.start)

    def arrive(messages):
        for side, copy in messages:
            pl.when(there(opposite(side)))(copy.wait_recv)

    def sent(messages):
        for side, copy in messages:
            pl.when(there(side))(copy.wait_send)

    own = pl.ds(ROW, Y)

    def thick(buf):
        return [
            message((1, 0), buf.at[pl.ds(Z, 2), own], buf.at[pl.ds(0, 2), own]),
            message((-1, 0), buf.at[pl.ds(2, 2), own], buf.at[pl.ds(Z + 2, 2), own]),
        ]

    def thin(buf):
        return [
            message((1, 0), buf.at[pl.ds(Z, 1), own], buf.at[pl.ds(0, 1), own]),
            message((-1, 0), buf.at[pl.ds(1, 1), own], buf.at[pl.ds(Z + 1, 1), own]),
        ]

    def along_y(src, dst):
        return [
            message((0, 1), src.at[1], dst.at[0]),
            message((0, -1), src.at[0], dst.at[1]),
        ]

    def corners(src, dst):
        return [message(side, src.at[i], dst.at[i]) for i, side in enumerate(SIDES[4:])]

    row = lax.broadcasted_iota(jnp.int32, (8, X), 0)
    col = lax.broadcasted_iota(jnp.int32, (8, X), 1)
    first, last = col == 0, col == X - 1
    lane = lax.broadcasted_iota(jnp.int32, (8, 128), 1)

    def left(x, fill=0.0):
        return jnp.where(first, fill, pltpu.roll(x, 1, 1))

    def right(x, fill=0.0):
        return jnp.where(last, fill, pltpu.roll(x, X - 1, 1))

    def rows(t, shift=0):
        return pl.ds(ROW + 8 * t + shift, 8)

    def pack(src, base, deep, dst, at):
        for z in range(Z):
            for k in range(deep):
                dst[0, at + k, pl.ds(z, 1), :] = src[base + z, pl.ds(ROW + k, 1), :]
                dst[1, at + k, pl.ds(z, 1), :] = src[base + z, pl.ds(ROW + Y - 1 - k, 1), :]

    def unpack(src, at, dst, base):
        for z in range(Z):
            dst[base + z, pl.ds(ROW - 1, 1), :] = src[0, at, pl.ds(z, 1), :]
            dst[base + z, pl.ds(ROW + Y, 1), :] = src[1, at, pl.ds(z, 1), :]

    def pack_corner(src, dst, at):
        for i, (sz, sy) in enumerate(SIDES[4:]):
            zc = Z + 1 if sz > 0 else 2
            yc = ROW + Y - 1 if sy > 0 else ROW
            dst[i, at] = src[zc, pl.ds(yc, 1), :]

    def unpack_corner(src, at, dst):
        for i, (sz, sy) in enumerate(SIDES[4:]):
            zc = 1 if sz > 0 else Z + 2
            yc = ROW - 1 if sy > 0 else ROW + Y
            dst[zc, pl.ds(yc, 1), :] = src[i, at]

    def diffs(buf, zc, t):
        c = buf[zc, rows(t), :]
        dz = buf[zc + 1, rows(t), :] - buf[zc - 1, rows(t), :]
        dy = buf[zc, rows(t, 1), :] - buf[zc, rows(t, -1), :]
        dx = right(c) - left(c)
        return c, dz, dy, dx

    def ring_diffs(buf, at, edge, edge_at, corner, corner_at, s):
        near, far, mine = buf[s, at], buf[s, at + 1], edge[s, edge_at]
        sy = 1 if s == 0 else -1
        lo = corner[SIDES[4:].index((1, sy)), corner_at]
        hi = corner[SIDES[4:].index((-1, sy)), corner_at]
        up = jnp.where(row == Z - 1, hi, pltpu.roll(near, Z - 1, 0))
        dn = jnp.where(row == 0, lo, pltpu.roll(near, 1, 0))
        dy = mine - far if s == 0 else far - mine
        return up - dn, dy, right(near) - left(near)

    def ends(c):
        return jnp.where(
            lane == 0, c[:, :128], jnp.where(lane == 127, c[:, X - 128:], 0.0)
        )

    def spread(e):
        return jnp.concatenate([e] * (X // 128), axis=1)

    def diff_flux(f, end):
        end = spread(end)
        return right(f, -end) - left(f, end)

    def end_basis(c):
        d = ends(c)
        xx = d * d
        r = recip(xx + FLOOR)
        qs = xx * xx * r
        q = qs * r
        a = BASE + RISE * q
        return d, xx, r, qs, q, a, a * (HALF_BASE - FALL * q), TWIST * a * r

    def end_flux(b):
        d, xx, r, qs, q, a, big_a, big_b = b
        return d * (big_a + big_b * xx)

    def end_tangent(b, e):
        d, xx, r, qs, q, a, big_a, big_b = b
        m = d * e
        dq = (4.0 * r * r) * (xx * m - qs * m)
        d_a = (SLOPE_0 + SLOPE_1 * q) * dq
        d_b = r * (TWIST * RISE * dq - (2.0 * TWIST) * a * r * m)
        return (big_a + 3.0 * big_b * xx) * e + d * (d_a + d_b * xx)

    def divergence(fz, fy, fx, z, t):
        total = fz[z + 2, pl.ds(8 * t, 8), :] - fz[z, pl.ds(8 * t, 8), :]
        total += fy[z, rows(t, 1), :] - fy[z, rows(t, -1), :]
        return 0.25 * (total + fx[z, pl.ds(8 * t, 8), :])

    def laplacian(buf, zc, t):
        c = buf[zc, rows(t), :]
        total = buf[zc + 1, rows(t), :] + buf[zc - 1, rows(t), :]
        total += buf[zc, rows(t, 1), :] + buf[zc, rows(t, -1), :]
        return c, total + right(c) + left(c) - 6.0 * c

    def reaction(p, u):
        x = DRIVE_SHARP * (MELT_POINT - u)
        m = DRIVE_SCALE / math.pi * arctan(x)
        well = p * (1.0 - p)
        tilt = p - 0.5 + m
        slope = (-DRIVE_SHARP * DRIVE_SCALE / math.pi) * recip(1.0 + x * x)
        return well * tilt, (1.0 - 2.0 * p) * tilt + well, well * slope

    def over_z(body):
        def step(z, carry):
            for t in tiles:
                body(z, t)
            return carry
        lax.fori_loop(0, Z, step, 0)

    def cells(t):
        return pl.ds(8 * t, 8)

    m_p0 = thick(p0)
    m_y0 = along_y(sy0, ry0)
    m_c0 = corners(sc0, rc0)
    m_u0 = thin(u0)
    m_d1 = thick(d1)
    m_t1 = thin(t1)
    m_y1 = along_y(sy1, ry1)
    m_p1 = thick(p1)
    m_y2 = along_y(sy2, ry2)
    m_c1 = corners(sc1, rc1)
    m_d0 = thick(d0)
    m_t0 = thin(t0)
    m_y3 = along_y(sy3, ry3)
    m_c2 = corners(sc2, rc2)

    def load(z, t):
        p0[z + 2, rows(t), :] = p_in[z, cells(t), :]
        u0[z + 1, rows(t), :] = u_in[z, cells(t), :]
        ts = ts_in[z, cells(t), :]
        t1[z + 1, rows(t), :] = ts
        w = ps_in[z, cells(t), :] + LATENT_HEAT * ts
        d1[z + 2, rows(t), :] = TIME_STEP * k_in[z, cells(t), :] * w
    over_z(load)
    pack(p0, 2, 2, sy0, 0)
    pack(u0, 1, 1, sy0, 2)
    pack_corner(p0, sc0, 0)
    pack_corner(d1, sc0, 1)
    pack(d1, 2, 2, sy1, 0)
    pack(t1, 1, 1, sy1, 2)

    @pl.when(zi == 0)
    def _():
        for buf in (p0, p1, d1, d0):
            buf[pl.ds(0, 2)] = jnp.zeros((2,) + buf.shape[1:], jnp.float32)
        for buf in (u0, t1, t0):
            buf[0] = jnp.zeros(buf.shape[1:], jnp.float32)

    @pl.when(zi == nz - 1)
    def _():
        for buf in (p0, p1, d1, d0):
            buf[pl.ds(Z + 2, 2)] = jnp.zeros((2,) + buf.shape[1:], jnp.float32)
        for buf in (u0, t1, t0):
            buf[Z + 1] = jnp.zeros(buf.shape[1:], jnp.float32)

    for s, at_end in ((0, yi == 0), (1, yi == ny - 1)):
        @pl.when(at_end)
        def _(s=s):
            for buf in (ry0, ry1, ry2, ry3):
                buf[s] = jnp.zeros(buf.shape[1:], jnp.float32)

    for i, side in enumerate(SIDES[4:]):
        @pl.when(jnp.logical_not(there(opposite(side))))
        def _(i=i):
            for buf in (rc0, rc1, rc2):
                buf[i] = jnp.zeros(buf.shape[1:], jnp.float32)

    def one(cond):
        return jnp.where(cond, 1, 0)

    near_z = one(zi > 0) + one(zi < nz - 1)
    near_y = one(yi > 0) + one(yi < ny - 1)
    pl.semaphore_wait(barrier, near_z + near_y + near_z * near_y)
    start(m_y0 + m_p0 + m_c0 + m_u0 + m_y1 + m_d1 + m_t1)

    def first_terms(z, t):
        p, u = p_in[z, cells(t), :], u_in[z, cells(t), :]
        r0[z, cells(t), :], rp0[z, cells(t), :], ru0[z, cells(t), :] = reaction(p, u)
    over_z(first_terms)

    arrive(m_y0 + m_c0)
    unpack(ry0, 0, p0, 2)
    unpack(ry0, 2, u0, 1)
    unpack_corner(rc0, 0, p0)
    arrive(m_p0 + m_u0)

    def put_ring(f, s, dst):
        at = ROW - 1 if s == 0 else ROW + Y
        for z in range(Z):
            dst[z, pl.ds(at, 1), :] = f[z:z + 1, :]

    def forward_flux(buf, zc, t):
        c, dz, dy, dx = diffs(buf, zc, t)
        b = basis(dz, dy, dx)
        return c, (dz, dy, dx), b

    def flux0(z, t):
        c, (dz, dy, dx), b = forward_flux(p0, z + 2, t)
        jz[z + 1, cells(t), :] = flux_of(dz, b[0], b)
        jy[z, rows(t), :] = flux_of(dy, b[1], b)
        jx[z, cells(t), :] = diff_flux(flux_of(dx, b[2], b), end_flux(end_basis(c)))
    over_z(flux0)
    for zc in (1, Z + 2):
        for t in tiles:
            _, (dz, dy, dx), b = forward_flux(p0, zc, t)
            jz[zc - 1, cells(t), :] = flux_of(dz, b[0], b)
    for s in (0, 1):
        dz, dy, dx = ring_diffs(ry0, 0, sy0, 0, rc0, 0, s)
        b = basis(dz, dy, dx)
        put_ring(flux_of(dy, b[1], b), s, jy)

    def advance(z, t):
        growth = divergence(jz, jy, jx, z, t) + r0[z, cells(t), :]
        gr0[z, cells(t), :] = growth
        p = p_in[z, cells(t), :]
        gain = TIME_STEP * k_in[z, cells(t), :] * growth
        p1[z + 2, rows(t), :] = p + gain
        u, lap = laplacian(u0, z + 1, t)
        u1[z, cells(t), :] = u + TIME_STEP * lap + LATENT_HEAT * gain
    over_z(advance)
    pack(p1, 2, 2, sy2, 0)
    pack_corner(p1, sc1, 0)
    start(m_y2 + m_p1 + m_c1)

    arrive(m_y1 + m_d1 + m_t1)
    unpack(ry1, 0, d1, 2)
    unpack(ry1, 2, t1, 1)
    unpack_corner(rc0, 1, d1)

    def second_terms(z, t):
        p, u = p1[z + 2, rows(t), :], u1[z, cells(t), :]
        r1[z, cells(t), :], rp1[z, cells(t), :], ru1[z, cells(t), :] = reaction(p, u)
        ts, lap = laplacian(t1, z + 1, t)
        tl1[z, cells(t), :] = ts + TIME_STEP * lap
    over_z(second_terms)

    arrive(m_y2 + m_c1)
    unpack(ry2, 0, p1, 2)
    unpack_corner(rc1, 0, p1)
    arrive(m_p1)

    def adjoint_flux(p, d, with_flux):
        def body(z, t):
            c, (dz, dy, dx), b = forward_flux(p, z + 2, t)
            e, ez, ey, ex = diffs(d, z + 2, t)
            k = tangent(dz, dy, dx, ez, ey, ex, b)
            eb = end_basis(c)
            gz[z + 1, cells(t), :] = turn(dz, b[0], ez, k)
            gy[z, rows(t), :] = turn(dy, b[1], ey, k)
            gx[z, cells(t), :] = diff_flux(turn(dx, b[2], ex, k), end_tangent(eb, ends(e)))
            if with_flux:
                jz[z + 1, cells(t), :] = flux_of(dz, b[0], b)
                jy[z, rows(t), :] = flux_of(dy, b[1], b)
                jx[z, cells(t), :] = diff_flux(flux_of(dx, b[2], b), end_flux(eb))
        over_z(body)
        for zc in (1, Z + 2):
            for t in tiles:
                _, (dz, dy, dx), b = forward_flux(p, zc, t)
                _, ez, ey, ex = diffs(d, zc, t)
                k = tangent(dz, dy, dx, ez, ey, ex, b)
                gz[zc - 1, cells(t), :] = turn(dz, b[0], ez, k)
                if with_flux:
                    jz[zc - 1, cells(t), :] = flux_of(dz, b[0], b)

    def adjoint_ring(p_args, d_args, with_flux):
        for s in (0, 1):
            dz, dy, dx = ring_diffs(*p_args, s)
            ez, ey, ex = ring_diffs(*d_args, s)
            b = basis(dz, dy, dx)
            k = tangent(dz, dy, dx, ez, ey, ex, b)
            put_ring(turn(dy, b[1], ey, k), s, gy)
            if with_flux:
                put_ring(flux_of(dy, b[1], b), s, jy)

    adjoint_flux(p1, d1, True)
    adjoint_ring((ry2, 0, sy2, 0, rc1, 0), (ry1, 0, sy1, 0, rc0, 1), True)

    def middle(z, t):
        d = d1[z + 2, rows(t), :]
        pb = ps_in[z, cells(t), :] + d * rp1[z, cells(t), :] + divergence(gz, gy, gx, z, t)
        ub = tl1[z, cells(t), :] + d * ru1[z, cells(t), :]
        pb0[z, cells(t), :] = pb
        t0[z + 1, rows(t), :] = ub
        d0[z + 2, rows(t), :] = TIME_STEP * k_in[z, cells(t), :] * (pb + LATENT_HEAT * ub)
    over_z(middle)
    pack(d0, 2, 2, sy3, 0)
    pack(t0, 1, 1, sy3, 2)
    pack_corner(d0, sc2, 0)
    start(m_y3 + m_d0 + m_c2 + m_t0)

    def mobility(z, t):
        growth = divergence(jz, jy, jx, z, t) + r1[z, cells(t), :]
        late = ps_in[z, cells(t), :] + LATENT_HEAT * ts_in[z, cells(t), :]
        early = pb0[z, cells(t), :] + LATENT_HEAT * t0[z + 1, rows(t), :]
        gm_out[z, cells(t), :] = TIME_STEP * (late * growth + early * gr0[z, cells(t), :])
    over_z(mobility)

    arrive(m_y3 + m_c2)
    unpack(ry3, 0, d0, 2)
    unpack(ry3, 2, t0, 1)
    unpack_corner(rc2, 0, d0)
    arrive(m_d0 + m_t0)
    adjoint_flux(p0, d0, False)
    adjoint_ring((ry0, 0, sy0, 0, rc0, 0), (ry3, 0, sy3, 0, rc2, 0), False)

    def finish(z, t):
        d = d0[z + 2, rows(t), :]
        sp_out[z, cells(t), :] = (
            pb0[z, cells(t), :] + d * rp0[z, cells(t), :] + divergence(gz, gy, gx, z, t)
        )
        ub, lap = laplacian(t0, z + 1, t)
        st_out[z, cells(t), :] = ub + TIME_STEP * lap + d * ru0[z, cells(t), :]
    over_z(finish)

    sent(
        m_p0 + m_y0 + m_c0 + m_u0 + m_d1 + m_t1 + m_y1
        + m_p1 + m_y2 + m_c1 + m_d0 + m_t0 + m_y3 + m_c2
    )


def body(nz, ny, *blocks):
    Z, Y, X = blocks[0].shape

    def buf(*shape):
        return pltpu.VMEM(shape, jnp.float32)

    wide = Y + 2 * ROW
    thick, thin, flat = (Z + 4, wide, X), (Z + 2, wide, X), (Z, Y, X)
    flux = [(Z + 2, Y, X), (Z, wide, X), (Z, Y, X)]
    scratch = [buf(*thick)] * 4 + [buf(*thin)] * 3 + [buf(*flat)]
    scratch += [buf(*s) for s in flux] * 2
    scratch += [buf(*flat)] * 9
    scratch += [buf(2, n, Z, X) for n in (3, 3, 3, 3, 2, 2, 3, 3)]
    scratch += [buf(4, n, 1, X) for n in (2, 2, 1, 1, 1, 1)]
    count = 36
    scratch += [pltpu.SemaphoreType.DMA((count,))] * 2
    vmem = pl.BlockSpec(memory_space=pltpu.VMEM)
    out = jax.ShapeDtypeStruct((Z, Y, X), jnp.float32)
    return pl.pallas_call(
        functools.partial(kernel, nz, ny),
        out_shape=(out, out, out),
        in_specs=[vmem] * 5,
        out_specs=(vmem, vmem, vmem),
        scratch_shapes=scratch,
        compiler_params=pltpu.CompilerParams(
            collective_id=0, has_side_effects=True, vmem_limit_bytes=40 * 1024 * 1024
        ),
    )(*blocks)


def solution(mesh):
    spec = P("gz", "gy", None)
    return jax.shard_map(
        functools.partial(body, mesh.shape["gz"], mesh.shape["gy"]),
        mesh=mesh,
        in_specs=(spec,) * 5,
        out_specs=(spec,) * 3,
        check_vma=False,
    )
```

```python
import functools
import math

import jax
import jax.numpy as jnp
from jax import lax
from jax.experimental import pallas as pl
from jax.experimental.pallas import tpu as pltpu
from jax.sharding import PartitionSpec as P

TIME_STEP = 0.15
ANISOTROPY = 0.05
GRAD_FLOOR = 0.01
LATENT_HEAT = 1.8
DRIVE_SCALE = 0.9
DRIVE_SHARP = 10.0
MELT_POINT = 1.0

BASE = 1.0 - 3.0 * ANISOTROPY
RISE = 4.0 * ANISOTROPY
HALF_BASE = 0.5 * BASE
FALL = 8.0 * ANISOTROPY - 0.5 * RISE
TWIST = 8.0 * ANISOTROPY
SLOPE_0 = RISE * HALF_BASE - FALL * BASE
SLOPE_1 = -2.0 * RISE * FALL
FLOOR = 4.0 * GRAD_FLOOR

ATAN = (
    1.0, -0.3333328366279602, 0.19998230040073395, -0.14261573553085327,
    0.10940198600292206, -0.08372063934803009, 0.05746355652809143,
    -0.030717508867383003, 0.010680719278752804, -0.0017437011701986194,
)

SIDES = ((1, 0), (-1, 0), (0, 1), (0, -1), (1, 1), (1, -1), (-1, 1), (-1, -1))


def recip(x):
    r = pl.reciprocal(x, approx=True)
    return r * (2.0 - x * r)


def arctan(x):
    size = jnp.abs(x)
    big = size > 1.0
    y = jnp.where(big, recip(jnp.maximum(size, 1.0)), size)
    z = y * y
    total = jnp.full_like(z, ATAN[-1])
    for c in ATAN[-2::-1]:
        total = total * z + c
    total = total * y
    total = jnp.where(big, 0.5 * math.pi - total, total)
    return jnp.where(x < 0.0, -total, total)


def basis(dz, dy, dx):
    zz, yy, xx = dz * dz, dy * dy, dx * dx
    s = zz + yy + xx + FLOOR
    r = recip(s)
    qs = (zz * zz + yy * yy + xx * xx) * r
    q = qs * r
    a = BASE + RISE * q
    big_a = a * (HALF_BASE - FALL * q)
    big_b = TWIST * a * r
    return zz, yy, xx, r, qs, q, a, big_a, big_b


def flux_of(d, sq, b):
    return d * (b[7] + b[8] * sq)


def tangent(dz, dy, dx, ez, ey, ex, b):
    zz, yy, xx, r, qs, q, a, big_a, big_b = b
    mz, my, mx = dz * ez, dy * ey, dx * ex
    g = mz + my + mx
    t = zz * mz + yy * my + xx * mx
    dq = (4.0 * r * r) * (t - qs * g)
    d_a = (SLOPE_0 + SLOPE_1 * q) * dq
    d_b = r * (TWIST * RISE * dq - (2.0 * TWIST) * a * r * g)
    return big_a, 3.0 * big_b, d_a, d_b


def turn(d, sq, e, t):
    return (t[0] + t[1] * sq) * e + d * (t[2] + t[3] * sq)


def kernel(
    nz, ny,
    p_in, u_in, k_in, ps_in, ts_in,
    sp_out, st_out, gm_out,
    p0, p1, d1, d0, u0, t1, t0, u1, kb, sb,
    jz, jxy, gz, gxy,
    r0, rp0, ru0, r1, rp1, ru1, tl1, gr0, pb0,
    ring_j, ring_g,
    sy0, ry0, sy1, ry1, sy2, ry2, sy3, ry3,
    sc0, rc0, sc1, rc1, sc2, rc2, sc3, rc3,
    ssem, rsem, lsem,
):
    Z, Y, X = p_in.shape
    T, C = Y // 8, X // 128
    zi, yi = lax.axis_index("gz"), lax.axis_index("gy")

    def there(side):
        cond = None
        for step, at, count in ((side[0], zi, nz), (side[1], yi, ny)):
            if step:
                c = at < count - 1 if step > 0 else at > 0
                cond = c if cond is None else jnp.logical_and(cond, c)
        return cond

    def opposite(side):
        return (-side[0], -side[1])

    barrier = pltpu.get_barrier_semaphore()
    for side in SIDES:
        @pl.when(there(side))
        def _(side=side):
            pl.semaphore_signal(
                barrier, inc=1, device_id=(zi + side[0], yi + side[1]),
                device_id_type=pl.DeviceIdType.MESH,
            )

    local = [
        pltpu.make_async_copy(src, dst, lsem.at[i])
        for i, (src, dst) in enumerate((
            (p_in, p0.at[pl.ds(2, Z)]),
            (k_in, kb),
            (ps_in, sb),
            (ts_in, t1.at[pl.ds(1, Z)]),
            (u_in, u0.at[pl.ds(1, Z)]),
        ))
    ]
    for copy in local:
        copy.start()

    slots = iter(range(1000))

    def message(side, src, dst):
        slot = next(slots)
        copy = pltpu.make_async_remote_copy(
            src_ref=src, dst_ref=dst, send_sem=ssem.at[slot], recv_sem=rsem.at[slot],
            device_id=(zi + side[0], yi + side[1]), device_id_type=pl.DeviceIdType.MESH,
        )
        return side, copy

    def start(messages):
        for side, copy in messages:
            pl.when(there(side))(copy.start)

    def arrive(messages):
        for side, copy in messages:
            pl.when(there(opposite(side)))(copy.wait_recv)

    def sent(messages):
        for side, copy in messages:
            pl.when(there(side))(copy.wait_send)

    def thick(buf):
        return [
            message((1, 0), buf.at[pl.ds(Z, 2)], buf.at[pl.ds(0, 2)]),
            message((-1, 0), buf.at[pl.ds(2, 2)], buf.at[pl.ds(Z + 2, 2)]),
        ]

    def thin(buf):
        return [
            message((1, 0), buf.at[pl.ds(Z, 1)], buf.at[pl.ds(0, 1)]),
            message((-1, 0), buf.at[pl.ds(1, 1)], buf.at[pl.ds(Z + 1, 1)]),
        ]

    def along_y(src, dst):
        return [
            message((0, 1), src.at[1], dst.at[0]),
            message((0, -1), src.at[0], dst.at[1]),
        ]

    def corners(src, dst):
        return [message(side, src.at[i], dst.at[i]) for i, side in enumerate(SIDES[4:])]

    lane = lax.broadcasted_iota(jnp.int32, (8, 128), 1)
    row = lax.broadcasted_iota(jnp.int32, (8, 128), 0)
    top, bottom = row == 0, row == 7
    first, last = lane == 0, lane == 127

    def block(j):
        return pl.ds(128 * j, 128)

    def layer(buf, z):
        return [[buf[z, pl.ds(8 * t, 8), block(j)] for j in range(C)] for t in range(T)]

    def store(buf, z, t, j, value):
        buf[z, pl.ds(8 * t, 8), block(j)] = value

    def wide_row(buf, *at):
        return [
            jnp.broadcast_to(buf[(*at[:-1], pl.ds(at[-1], 1), block(j))], (8, 128))
            for j in range(C)
        ]

    def shift_x(row_of_tiles, end=None):
        before = [pltpu.roll(c, 1, 1) for c in row_of_tiles]
        after = [pltpu.roll(c, 127, 1) for c in row_of_tiles]
        zero = 0.0
        lo = [
            jnp.where(first, before[j - 1] if j else (zero if end is None else end), before[j])
            for j in range(C)
        ]
        hi = [
            jnp.where(
                last, after[j + 1] if j < C - 1 else (zero if end is None else -end), after[j]
            )
            for j in range(C)
        ]
        return lo, hi

    def shift_y(tiles, lo, hi):
        before = [[pltpu.roll(c, 1, 0) for c in r] for r in tiles]
        after = [[pltpu.roll(c, 7, 0) for c in r] for r in tiles]
        down = [
            [jnp.where(top, before[t - 1][j] if t else lo[j], before[t][j]) for j in range(C)]
            for t in range(T)
        ]
        up = [
            [jnp.where(bottom, after[t + 1][j] if t < T - 1 else hi[j], after[t][j]) for j in range(C)]
            for t in range(T)
        ]
        return down, up

    def sub(a, b):
        if isinstance(a, list):
            return [sub(x, y) for x, y in zip(a, b)]
        return a - b

    def diffs(buf, zc, lo, hi):
        c = layer(buf, zc)
        dz = sub(layer(buf, zc + 1), layer(buf, zc - 1))
        down, up = shift_y(c, lo, hi)
        sides = [shift_x(r) for r in c]
        return c, dz, sub(up, down), [sub(h, l) for l, h in sides]

    def halo_rows(rim, at, z):
        at = () if at is None else (at,)
        lo = [pltpu.roll(rim[(0, *at, slice(None), block(j))], lax.rem(Z - z, 8), 0) for j in range(C)]
        hi = [pltpu.roll(rim[(1, *at, slice(None), block(j))], 7 - z, 0) for j in range(C)]
        return lo, hi

    def corner_rows(corner, at, below):
        sz = 1 if below else -1
        lo = SIDES[4:].index((sz, 1))
        hi = SIDES[4:].index((sz, -1))
        return wide_row(corner, lo, at, 0), wide_row(corner, hi, at, 0)

    def ring_diffs(rim, at, edge, edge_at, corner, corner_at, s):
        near = [rim[s, at, :, block(j)] for j in range(C)]
        far = [rim[s, at + 1, :, block(j)] for j in range(C)]
        mine = [edge[s, edge_at, :, block(j)] for j in range(C)]
        sy = 1 if s == 0 else -1
        lo = wide_row(corner, SIDES[4:].index((1, sy)), corner_at, 0)
        hi = wide_row(corner, SIDES[4:].index((-1, sy)), corner_at, 0)
        (dn,), (up,) = ring_shift(near, lo, hi)
        l, h = shift_x(near)
        dy = sub(mine, far) if s == 0 else sub(far, mine)
        return sub(up, dn), dy, sub(h, l)

    def ring_shift(near, lo, hi):
        down = [jnp.where(top, lo[j], pltpu.roll(near[j], 1, 0)) for j in range(C)]
        up = [jnp.where(bottom, hi[j], pltpu.roll(near[j], 7, 0)) for j in range(C)]
        return [down], [up]

    def pack(src, base, deep, dst, at):
        for k in range(deep):
            for s, y in ((0, k), (1, Y - 1 - k)):
                total = wide_row(src, base, y)
                for z in range(1, Z):
                    now = wide_row(src, base + z, y)
                    total = [jnp.where(row == z, n, o) for n, o in zip(now, total)]
                for j in range(C):
                    dst[s, at + k, :, block(j)] = total[j]

    def pack_corner(src, dst):
        for i, (sz, sy) in enumerate(SIDES[4:]):
            zc = Z + 1 if sz > 0 else 2
            yc = Y - 1 if sy > 0 else 0
            dst[i, 0] = src[zc, pl.ds(yc, 1), :]

    def ends(tiles):
        return jnp.where(first, tiles[0], jnp.where(last, tiles[C - 1], 0.0))

    def end_basis(d):
        xx = d * d
        r = recip(xx + FLOOR)
        qs = xx * xx * r
        q = qs * r
        a = BASE + RISE * q
        return d, xx, r, qs, q, a, a * (HALF_BASE - FALL * q), TWIST * a * r

    def end_flux(b):
        d, xx, r, qs, q, a, big_a, big_b = b
        return d * (big_a + big_b * xx)

    def end_tangent(b, e):
        d, xx, r, qs, q, a, big_a, big_b = b
        m = d * e
        dq = (4.0 * r * r) * (xx * m - qs * m)
        d_a = (SLOPE_0 + SLOPE_1 * q) * dq
        d_b = r * (TWIST * RISE * dq - (2.0 * TWIST) * a * r * m)
        return (big_a + 3.0 * big_b * xx) * e + d * (d_a + d_b * xx)

    def cross(fx, fy, end, lo, hi):
        out = []
        down, up = shift_y(fy, lo, hi)
        for t in range(T):
            l, h = shift_x(fx[t], end[t])
            out.append([(h[j] - l[j]) + (up[t][j] - down[t][j]) for j in range(C)])
        return out

    def blank():
        return [[None] * C for _ in range(T)]

    def flux_layer(p, zc, p_rows, d=None, d_rows=None, with_flux=True, ring=None):
        c, dz, dy, dx = diffs(p, zc, *p_rows)
        if d is not None:
            e, ez, ey, ex = diffs(d, zc, *d_rows)
        fx, fy, hx, hy = blank(), blank(), blank(), blank()
        for t in range(T):
            for j in range(C):
                a = (dz[t][j], dy[t][j], dx[t][j])
                b = basis(*a)
                if with_flux:
                    store(jz, zc - 1, t, j, flux_of(a[0], b[0], b))
                    if ring is not None:
                        fy[t][j] = flux_of(a[1], b[1], b)
                        fx[t][j] = flux_of(a[2], b[2], b)
                if d is not None:
                    v = (ez[t][j], ey[t][j], ex[t][j])
                    k = tangent(*a, *v, b)
                    store(gz, zc - 1, t, j, turn(a[0], b[0], v[0], k))
                    if ring is not None:
                        hy[t][j] = turn(a[1], b[1], v[1], k)
                        hx[t][j] = turn(a[2], b[2], v[2], k)
        if ring is None:
            return
        eb = [end_basis(ends(r)) for r in c]
        if with_flux:
            rows = halo_rows(ring_j, None, ring)
            out = cross(fx, fy, [end_flux(b) for b in eb], *rows)
            for t in range(T):
                for j in range(C):
                    store(jxy, ring, t, j, out[t][j])
        if d is not None:
            rows = halo_rows(ring_g, None, ring)
            out = cross(hx, hy, [end_tangent(b, ends(r)) for b, r in zip(eb, e)], *rows)
            for t in range(T):
                for j in range(C):
                    store(gxy, ring, t, j, out[t][j])

    def flux_ring(p_args, d_args=None, with_flux=True):
        for s in (0, 1):
            dz, dy, dx = ring_diffs(*p_args, s)
            if d_args is not None:
                ez, ey, ex = ring_diffs(*d_args, s)
            for j in range(C):
                b = basis(dz[j], dy[j], dx[j])
                if with_flux:
                    ring_j[s, :, block(j)] = flux_of(dy[j], b[1], b)
                if d_args is not None:
                    k = tangent(dz[j], dy[j], dx[j], ez[j], ey[j], ex[j], b)
                    ring_g[s, :, block(j)] = turn(dy[j], b[1], ey[j], k)

    def divergence(fz, fxy, z, t, j):
        at = (pl.ds(8 * t, 8), block(j))
        return 0.25 * ((fz[(z + 2, *at)] - fz[(z, *at)]) + fxy[(z, *at)])

    def laplacian(buf, zc, lo, hi):
        c, below, above = layer(buf, zc), layer(buf, zc - 1), layer(buf, zc + 1)
        down, up = shift_y(c, lo, hi)
        out = blank()
        for t in range(T):
            l, h = shift_x(c[t])
            for j in range(C):
                total = (below[t][j] + above[t][j]) + (down[t][j] + up[t][j])
                out[t][j] = c[t][j] + TIME_STEP * (total + (l[j] + h[j]) - 6.0 * c[t][j])
        return out

    def reaction(p, u):
        x = DRIVE_SHARP * (MELT_POINT - u)
        m = DRIVE_SCALE / math.pi * arctan(x)
        well = p * (1.0 - p)
        tilt = p - 0.5 + m
        slope = (-DRIVE_SHARP * DRIVE_SCALE / math.pi) * recip(1.0 + x * x)
        return well * tilt, (1.0 - 2.0 * p) * tilt + well, well * slope

    def over(lo, hi, body, step=1):
        def one_layer(i, carry):
            body(lo + i * step)
            return carry
        lax.fori_loop(0, (hi - lo + step - 1) // step, one_layer, 0)

    def inner(body):
        over(1, Z - 1, body)

    def outer(body):
        over(0, Z, body, Z - 1)

    def per_tile(body):
        def whole(z):
            for t in range(T):
                for j in range(C):
                    body(z, t, j)
        return whole

    def get(buf, z, t, j):
        return buf[z, pl.ds(8 * t, 8), block(j)]

    m_p0, m_y0, m_c0 = thick(p0), along_y(sy0, ry0), corners(sc0, rc0)
    m_u0, m_d1, m_t1 = thin(u0), thick(d1), thin(t1)
    m_y1, m_c1 = along_y(sy1, ry1), corners(sc1, rc1)
    m_p1, m_y2, m_c2 = thick(p1), along_y(sy2, ry2), corners(sc2, rc2)
    m_d0, m_t0 = thick(d0), thin(t0)
    m_y3, m_c3 = along_y(sy3, ry3), corners(sc3, rc3)

    @pl.when(zi == 0)
    def _():
        for buf in (p0, p1, d1, d0):
            buf[pl.ds(0, 2)] = jnp.zeros((2,) + buf.shape[1:], jnp.float32)
        for buf in (u0, t1, t0):
            buf[0] = jnp.zeros(buf.shape[1:], jnp.float32)

    @pl.when(zi == nz - 1)
    def _():
        for buf in (p0, p1, d1, d0):
            buf[pl.ds(Z + 2, 2)] = jnp.zeros((2,) + buf.shape[1:], jnp.float32)
        for buf in (u0, t1, t0):
            buf[Z + 1] = jnp.zeros(buf.shape[1:], jnp.float32)

    for s, at_end in ((0, yi == 0), (1, yi == ny - 1)):
        @pl.when(at_end)
        def _(s=s):
            for buf in (ry0, ry1, ry2, ry3):
                buf[s] = jnp.zeros(buf.shape[1:], jnp.float32)

    for i, side in enumerate(SIDES[4:]):
        @pl.when(jnp.logical_not(there(opposite(side))))
        def _(i=i):
            for buf in (rc0, rc1, rc2, rc3):
                buf[i] = jnp.zeros(buf.shape[1:], jnp.float32)

    def one(cond):
        return jnp.where(cond, 1, 0)

    local[0].wait()
    pack(p0, 2, 2, sy0, 0)
    pack_corner(p0, sc0)
    near_z = one(zi > 0) + one(zi < nz - 1)
    near_y = one(yi > 0) + one(yi < ny - 1)
    pl.semaphore_wait(barrier, near_z + near_y + near_z * near_y)
    start(m_y0 + m_c0 + m_p0)

    for copy in local[1:]:
        copy.wait()

    @per_tile
    def weight(z, t, j):
        w = get(sb, z, t, j) + LATENT_HEAT * get(t1, z + 1, t, j)
        store(d1, z + 2, t, j, TIME_STEP * get(kb, z, t, j) * w)
    over(0, Z, weight)
    pack(u0, 1, 1, sy1, 0)
    pack(d1, 2, 2, sy1, 1)
    pack(t1, 1, 1, sy1, 3)
    pack_corner(d1, sc1)
    start(m_y1 + m_c1 + m_u0 + m_d1 + m_t1)

    @per_tile
    def first_terms(z, t, j):
        a, b, c = reaction(get(p0, z + 2, t, j), get(u0, z + 1, t, j))
        store(r0, z, t, j, a)
        store(rp0, z, t, j, b)
        store(ru0, z, t, j, c)
    over(0, Z, first_terms)

    arrive(m_y0 + m_c0)
    flux_ring((ry0, 0, sy0, 0, rc0, 0))

    def flux0(z):
        flux_layer(p0, z + 2, halo_rows(ry0, 0, z), ring=z)
    inner(flux0)
    arrive(m_p0)
    outer(flux0)
    flux_layer(p0, 1, corner_rows(rc0, 0, True))
    flux_layer(p0, Z + 2, corner_rows(rc0, 0, False))

    @per_tile
    def advance(z, t, j):
        growth = divergence(jz, jxy, z, t, j) + get(r0, z, t, j)
        store(gr0, z, t, j, growth)
        gain = TIME_STEP * get(kb, z, t, j) * growth
        store(p1, z + 2, t, j, get(p0, z + 2, t, j) + gain)
    over(0, 2, advance)
    over(Z - 2, Z, advance)
    pack_corner(p1, sc2)
    start(m_c2 + m_p1)
    over(2, Z - 2, advance)
    pack(p1, 2, 2, sy2, 0)
    start(m_y2)

    arrive(m_y1 + m_c1 + m_u0 + m_d1 + m_t1)

    def second_terms(z):
        new_u = laplacian(u0, z + 1, *halo_rows(ry1, 0, z))
        new_t = laplacian(t1, z + 1, *halo_rows(ry1, 3, z))
        for t in range(T):
            for j in range(C):
                p = get(p1, z + 2, t, j)
                u = new_u[t][j] + LATENT_HEAT * (p - get(p0, z + 2, t, j))
                a, b, c = reaction(p, u)
                store(r1, z, t, j, a)
                store(rp1, z, t, j, b)
                store(ru1, z, t, j, c)
                store(tl1, z, t, j, new_t[t][j])
    over(0, Z, second_terms)

    arrive(m_y2 + m_c2)
    flux_ring((ry2, 0, sy2, 0, rc2, 0), (ry1, 1, sy1, 1, rc1, 0))

    def adjoint1(z):
        flux_layer(p1, z + 2, halo_rows(ry2, 0, z), d1, halo_rows(ry1, 1, z), ring=z)
    inner(adjoint1)
    arrive(m_p1)
    outer(adjoint1)
    flux_layer(p1, 1, corner_rows(rc2, 0, True), d1, corner_rows(rc1, 0, True))
    flux_layer(p1, Z + 2, corner_rows(rc2, 0, False), d1, corner_rows(rc1, 0, False))

    @per_tile
    def middle(z, t, j):
        d = get(d1, z + 2, t, j)
        pb = get(sb, z, t, j) + d * get(rp1, z, t, j) + divergence(gz, gxy, z, t, j)
        ub = get(tl1, z, t, j) + d * get(ru1, z, t, j)
        store(pb0, z, t, j, pb)
        store(t0, z + 1, t, j, ub)
        store(d0, z + 2, t, j, TIME_STEP * get(kb, z, t, j) * (pb + LATENT_HEAT * ub))
    over(0, 2, middle)
    over(Z - 2, Z, middle)
    pack_corner(d0, sc3)
    start(m_c3 + m_d0 + m_t0)
    over(2, Z - 2, middle)
    pack(d0, 2, 2, sy3, 0)
    pack(t0, 1, 1, sy3, 2)
    start(m_y3)

    @per_tile
    def mobility(z, t, j):
        growth = divergence(jz, jxy, z, t, j) + get(r1, z, t, j)
        late = get(sb, z, t, j) + LATENT_HEAT * get(t1, z + 1, t, j)
        early = get(pb0, z, t, j) + LATENT_HEAT * get(t0, z + 1, t, j)
        store(gm_out, z, t, j, TIME_STEP * (late * growth + early * get(gr0, z, t, j)))
    over(0, Z, mobility)

    arrive(m_y3 + m_c3)
    flux_ring((ry0, 0, sy0, 0, rc0, 0), (ry3, 0, sy3, 0, rc3, 0), False)

    def adjoint0(z):
        flux_layer(p0, z + 2, halo_rows(ry0, 0, z), d0, halo_rows(ry3, 0, z), False, ring=z)
    inner(adjoint0)
    arrive(m_d0 + m_t0)
    outer(adjoint0)
    flux_layer(p0, 1, corner_rows(rc0, 0, True), d0, corner_rows(rc3, 0, True), False)
    flux_layer(p0, Z + 2, corner_rows(rc0, 0, False), d0, corner_rows(rc3, 0, False), False)

    def finish(z):
        new_t = laplacian(t0, z + 1, *halo_rows(ry3, 2, z))
        for t in range(T):
            for j in range(C):
                d = get(d0, z + 2, t, j)
                pb = get(pb0, z, t, j) + d * get(rp0, z, t, j)
                store(sp_out, z, t, j, pb + divergence(gz, gxy, z, t, j))
                store(st_out, z, t, j, new_t[t][j] + d * get(ru0, z, t, j))
    over(0, Z, finish)

    sent(m_p0 + m_y0 + m_c0 + m_u0 + m_d1 + m_t1 + m_y1 + m_c1)
    sent(m_p1 + m_y2 + m_c2 + m_d0 + m_t0 + m_y3 + m_c3)


def body(nz, ny, *blocks):
    Z, Y, X = blocks[0].shape

    def buf(*shape):
        return pltpu.VMEM(shape, jnp.float32)

    thick, thin, flat = (Z + 4, Y, X), (Z + 2, Y, X), (Z, Y, X)
    scratch = [buf(*thick)] * 4 + [buf(*thin)] * 3 + [buf(*flat)] * 3
    scratch += [buf(*thin), buf(*flat)] * 2
    scratch += [buf(*flat)] * 9
    scratch += [buf(2, Z, X)] * 2
    scratch += [buf(2, n, Z, X) for n in (2, 2, 4, 4, 2, 2, 3, 3)]
    scratch += [buf(4, 1, 1, X)] * 8
    count = 38
    scratch += [pltpu.SemaphoreType.DMA((count,))] * 2 + [pltpu.SemaphoreType.DMA((5,))]
    vmem = pl.BlockSpec(memory_space=pltpu.VMEM)
    hbm = pl.BlockSpec(memory_space=pltpu.HBM)
    out = jax.ShapeDtypeStruct((Z, Y, X), jnp.float32)
    return pl.pallas_call(
        functools.partial(kernel, nz, ny),
        out_shape=(out, out, out),
        in_specs=[hbm] * 5,
        out_specs=(vmem, vmem, vmem),
        scratch_shapes=scratch,
        compiler_params=pltpu.CompilerParams(
            collective_id=0, has_side_effects=True, vmem_limit_bytes=40 * 1024 * 1024
        ),
    )(*blocks)


def solution(mesh):
    spec = P("gz", "gy", None)
    return jax.shard_map(
        functools.partial(body, mesh.shape["gz"], mesh.shape["gy"]),
        mesh=mesh,
        in_specs=(spec,) * 5,
        out_specs=(spec,) * 3,
        check_vma=False,
    )
```

```python
import functools
import math

import jax
import jax.numpy as jnp
from jax import lax
from jax.experimental import pallas as pl
from jax.experimental.pallas import tpu as pltpu
from jax.sharding import PartitionSpec as P

TIME_STEP = 0.15
ANISOTROPY = 0.05
GRAD_FLOOR = 0.01
LATENT_HEAT = 1.8
DRIVE_SCALE = 0.9
DRIVE_SHARP = 10.0
MELT_POINT = 1.0

BASE = 1.0 - 3.0 * ANISOTROPY
RISE = 4.0 * ANISOTROPY
HALF_BASE = 0.5 * BASE
FALL = 8.0 * ANISOTROPY - 0.5 * RISE
TWIST = 8.0 * ANISOTROPY
SLOPE_0 = RISE * HALF_BASE - FALL * BASE
SLOPE_1 = -2.0 * RISE * FALL
FLOOR = 4.0 * GRAD_FLOOR

ATAN = (
    1.0, -0.3333328366279602, 0.19998230040073395, -0.14261573553085327,
    0.10940198600292206, -0.08372063934803009, 0.05746355652809143,
    -0.030717508867383003, 0.010680719278752804, -0.0017437011701986194,
)

SIDES = ((1, 0), (-1, 0), (0, 1), (0, -1), (1, 1), (1, -1), (-1, 1), (-1, -1))


def recip(x):
    r = pl.reciprocal(x, approx=True)
    return r * (2.0 - x * r)


def arctan(x):
    size = jnp.abs(x)
    big = size > 1.0
    y = jnp.where(big, recip(jnp.maximum(size, 1.0)), size)
    z = y * y
    total = jnp.full_like(z, ATAN[-1])
    for c in ATAN[-2::-1]:
        total = total * z + c
    total = total * y
    total = jnp.where(big, 0.5 * math.pi - total, total)
    return jnp.where(x < 0.0, -total, total)


def basis(dz, dy, dx):
    zz, yy, xx = dz * dz, dy * dy, dx * dx
    s = zz + yy + xx + FLOOR
    r = recip(s)
    qs = (zz * zz + yy * yy + xx * xx) * r
    q = qs * r
    a = BASE + RISE * q
    big_a = a * (HALF_BASE - FALL * q)
    big_b = TWIST * a * r
    return zz, yy, xx, r, qs, q, a, big_a, big_b


def flux_of(d, sq, b):
    return d * (b[7] + b[8] * sq)


def tangent(dz, dy, dx, ez, ey, ex, b):
    zz, yy, xx, r, qs, q, a, big_a, big_b = b
    mz, my, mx = dz * ez, dy * ey, dx * ex
    g = mz + my + mx
    t = zz * mz + yy * my + xx * mx
    dq = (4.0 * r * r) * (t - qs * g)
    d_a = (SLOPE_0 + SLOPE_1 * q) * dq
    d_b = r * (TWIST * RISE * dq - (2.0 * TWIST) * a * r * g)
    return big_a, 3.0 * big_b, d_a, d_b


def turn(d, sq, e, t):
    return (t[0] + t[1] * sq) * e + d * (t[2] + t[3] * sq)


def kernel(
    nz, ny,
    p_in, u_in, k_in, ps_in, ts_in,
    sp_hbm, st_hbm, gm_hbm,
    sp_out, st_out, gm_out,
    p0, p1, d1, d0, u0, t1, t0, u1, kb, sb,
    jz, jxy, gz, gxy,
    r0, rp0, ru0, r1, rp1, ru1, tl1, gr0, pb0,
    ring_j, ring_g,
    sy0, ry0, sy1, ry1, sy2, ry2, sy3, ry3,
    sc0, rc0, sc1, rc1, sc2, rc2, sc3, rc3,
    ssem, rsem, lsem,
):
    Z, Y, X = p_in.shape
    T, C = Y // 8, X // 128
    zi, yi = lax.axis_index("gz"), lax.axis_index("gy")

    def there(side):
        cond = None
        for step, at, count in ((side[0], zi, nz), (side[1], yi, ny)):
            if step:
                c = at < count - 1 if step > 0 else at > 0
                cond = c if cond is None else jnp.logical_and(cond, c)
        return cond

    def opposite(side):
        return (-side[0], -side[1])

    barrier = pltpu.get_barrier_semaphore()
    for side in SIDES:
        @pl.when(there(side))
        def _(side=side):
            pl.semaphore_signal(
                barrier, inc=1, device_id=(zi + side[0], yi + side[1]),
                device_id_type=pl.DeviceIdType.MESH,
            )

    local = [
        pltpu.make_async_copy(src, dst, lsem.at[i])
        for i, (src, dst) in enumerate((
            (p_in, p0.at[pl.ds(2, Z)]),
            (k_in, kb),
            (ps_in, sb),
            (ts_in, t1.at[pl.ds(1, Z)]),
            (u_in, u0.at[pl.ds(1, Z)]),
        ))
    ]
    for copy in local:
        copy.start()

    slots = iter(range(1000))

    def message(side, src, dst):
        slot = next(slots)
        copy = pltpu.make_async_remote_copy(
            src_ref=src, dst_ref=dst, send_sem=ssem.at[slot], recv_sem=rsem.at[slot],
            device_id=(zi + side[0], yi + side[1]), device_id_type=pl.DeviceIdType.MESH,
        )
        return side, copy

    def start(messages):
        for side, copy in messages:
            pl.when(there(side))(copy.start)

    def arrive(messages):
        for side, copy in messages:
            pl.when(there(opposite(side)))(copy.wait_recv)

    def sent(messages):
        for side, copy in messages:
            pl.when(there(side))(copy.wait_send)

    def thick(buf):
        return [
            message((1, 0), buf.at[pl.ds(Z, 2)], buf.at[pl.ds(0, 2)]),
            message((-1, 0), buf.at[pl.ds(2, 2)], buf.at[pl.ds(Z + 2, 2)]),
        ]

    def thin(buf):
        return [
            message((1, 0), buf.at[pl.ds(Z, 1)], buf.at[pl.ds(0, 1)]),
            message((-1, 0), buf.at[pl.ds(1, 1)], buf.at[pl.ds(Z + 1, 1)]),
        ]

    def along_y(src, dst):
        return [
            message((0, 1), src.at[1], dst.at[0]),
            message((0, -1), src.at[0], dst.at[1]),
        ]

    def corners(src, dst):
        return [message(side, src.at[i], dst.at[i]) for i, side in enumerate(SIDES[4:])]

    lane = lax.broadcasted_iota(jnp.int32, (8, 128), 1)
    row = lax.broadcasted_iota(jnp.int32, (8, 128), 0)
    top, bottom = row == 0, row == 7
    first, last = lane == 0, lane == 127

    def block(j):
        return pl.ds(128 * j, 128)

    def layer(buf, z):
        return [[buf[z, pl.ds(8 * t, 8), block(j)] for j in range(C)] for t in range(T)]

    def store(buf, z, t, j, value):
        buf[z, pl.ds(8 * t, 8), block(j)] = value

    def wide_row(buf, *at):
        return [
            jnp.broadcast_to(buf[(*at[:-1], pl.ds(at[-1], 1), block(j))], (8, 128))
            for j in range(C)
        ]

    def shift_x(row_of_tiles, end=None):
        before = [pltpu.roll(c, 1, 1) for c in row_of_tiles]
        after = [pltpu.roll(c, 127, 1) for c in row_of_tiles]
        zero = 0.0
        lo = [
            jnp.where(first, before[j - 1] if j else (zero if end is None else end), before[j])
            for j in range(C)
        ]
        hi = [
            jnp.where(
                last, after[j + 1] if j < C - 1 else (zero if end is None else -end), after[j]
            )
            for j in range(C)
        ]
        return lo, hi

    def shift_y(tiles, lo, hi):
        before = [[pltpu.roll(c, 1, 0) for c in r] for r in tiles]
        after = [[pltpu.roll(c, 7, 0) for c in r] for r in tiles]
        down = [
            [jnp.where(top, before[t - 1][j] if t else lo[j], before[t][j]) for j in range(C)]
            for t in range(T)
        ]
        up = [
            [jnp.where(bottom, after[t + 1][j] if t < T - 1 else hi[j], after[t][j]) for j in range(C)]
            for t in range(T)
        ]
        return down, up

    def sub(a, b):
        if isinstance(a, list):
            return [sub(x, y) for x, y in zip(a, b)]
        return a - b

    def diffs(buf, zc, lo, hi):
        c = layer(buf, zc)
        dz = sub(layer(buf, zc + 1), layer(buf, zc - 1))
        down, up = shift_y(c, lo, hi)
        sides = [shift_x(r) for r in c]
        return c, dz, sub(up, down), [sub(h, l) for l, h in sides]

    def halo_rows(rim, at, z):
        at = () if at is None else (at,)
        if isinstance(z, int):
            return wide_row(rim, 0, *at, z), wide_row(rim, 1, *at, z)
        down = lax.rem(Z - z, 8)
        lo = [pltpu.roll(rim[(0, *at, slice(None), block(j))], down, 0) for j in range(C)]
        hi = [pltpu.roll(rim[(1, *at, slice(None), block(j))], 7 - z, 0) for j in range(C)]
        return lo, hi

    def corner_rows(corner, at, below):
        sz = 1 if below else -1
        lo = SIDES[4:].index((sz, 1))
        hi = SIDES[4:].index((sz, -1))
        return wide_row(corner, lo, at, 0), wide_row(corner, hi, at, 0)

    def ring_diffs(rim, at, edge, edge_at, corner, corner_at, s):
        near = [rim[s, at, :, block(j)] for j in range(C)]
        far = [rim[s, at + 1, :, block(j)] for j in range(C)]
        mine = [edge[s, edge_at, :, block(j)] for j in range(C)]
        sy = 1 if s == 0 else -1
        lo = wide_row(corner, SIDES[4:].index((1, sy)), corner_at, 0)
        hi = wide_row(corner, SIDES[4:].index((-1, sy)), corner_at, 0)
        (dn,), (up,) = ring_shift(near, lo, hi)
        l, h = shift_x(near)
        dy = sub(mine, far) if s == 0 else sub(far, mine)
        return sub(up, dn), dy, sub(h, l)

    def ring_shift(near, lo, hi):
        down = [jnp.where(top, lo[j], pltpu.roll(near[j], 1, 0)) for j in range(C)]
        up = [jnp.where(bottom, hi[j], pltpu.roll(near[j], 7, 0)) for j in range(C)]
        return [down], [up]

    def pack(src, base, deep, dst, at):
        for k in range(deep):
            for s, y in ((0, k), (1, Y - 1 - k)):
                total = wide_row(src, base, y)
                for z in range(1, Z):
                    now = wide_row(src, base + z, y)
                    total = [jnp.where(row == z, n, o) for n, o in zip(now, total)]
                for j in range(C):
                    dst[s, at + k, :, block(j)] = total[j]

    def pack_corner(src, dst):
        for i, (sz, sy) in enumerate(SIDES[4:]):
            zc = Z + 1 if sz > 0 else 2
            yc = Y - 1 if sy > 0 else 0
            dst[i, 0] = src[zc, pl.ds(yc, 1), :]

    def ends(tiles):
        return jnp.where(first, tiles[0], jnp.where(last, tiles[C - 1], 0.0))

    def end_basis(d):
        xx = d * d
        r = recip(xx + FLOOR)
        qs = xx * xx * r
        q = qs * r
        a = BASE + RISE * q
        return d, xx, r, qs, q, a, a * (HALF_BASE - FALL * q), TWIST * a * r

    def end_flux(b):
        d, xx, r, qs, q, a, big_a, big_b = b
        return d * (big_a + big_b * xx)

    def end_tangent(b, e):
        d, xx, r, qs, q, a, big_a, big_b = b
        m = d * e
        dq = (4.0 * r * r) * (xx * m - qs * m)
        d_a = (SLOPE_0 + SLOPE_1 * q) * dq
        d_b = r * (TWIST * RISE * dq - (2.0 * TWIST) * a * r * m)
        return (big_a + 3.0 * big_b * xx) * e + d * (d_a + d_b * xx)

    def cross(fx, fy, end, lo, hi):
        out = []
        down, up = shift_y(fy, lo, hi)
        for t in range(T):
            l, h = shift_x(fx[t], end[t])
            out.append([(h[j] - l[j]) + (up[t][j] - down[t][j]) for j in range(C)])
        return out

    def blank():
        return [[None] * C for _ in range(T)]

    def flux_layer(p, zc, p_rows, d=None, d_rows=None, with_flux=True, ring=None):
        c, dz, dy, dx = diffs(p, zc, *p_rows)
        if d is not None:
            e, ez, ey, ex = diffs(d, zc, *d_rows)
        fx, fy, hx, hy = blank(), blank(), blank(), blank()
        for t in range(T):
            for j in range(C):
                a = (dz[t][j], dy[t][j], dx[t][j])
                b = basis(*a)
                if with_flux:
                    store(jz, zc - 1, t, j, flux_of(a[0], b[0], b))
                    if ring is not None:
                        fy[t][j] = flux_of(a[1], b[1], b)
                        fx[t][j] = flux_of(a[2], b[2], b)
                if d is not None:
                    v = (ez[t][j], ey[t][j], ex[t][j])
                    k = tangent(*a, *v, b)
                    store(gz, zc - 1, t, j, turn(a[0], b[0], v[0], k))
                    if ring is not None:
                        hy[t][j] = turn(a[1], b[1], v[1], k)
                        hx[t][j] = turn(a[2], b[2], v[2], k)
        if ring is None:
            return
        eb = [end_basis(ends(r)) for r in c]
        if with_flux:
            rows = halo_rows(ring_j, None, ring)
            out = cross(fx, fy, [end_flux(b) for b in eb], *rows)
            for t in range(T):
                for j in range(C):
                    store(jxy, ring, t, j, out[t][j])
        if d is not None:
            rows = halo_rows(ring_g, None, ring)
            out = cross(hx, hy, [end_tangent(b, ends(r)) for b, r in zip(eb, e)], *rows)
            for t in range(T):
                for j in range(C):
                    store(gxy, ring, t, j, out[t][j])

    def flux_ring(p_args, d_args=None, with_flux=True):
        for s in (0, 1):
            dz, dy, dx = ring_diffs(*p_args, s)
            if d_args is not None:
                ez, ey, ex = ring_diffs(*d_args, s)
            for j in range(C):
                b = basis(dz[j], dy[j], dx[j])
                if with_flux:
                    ring_j[s, :, block(j)] = flux_of(dy[j], b[1], b)
                if d_args is not None:
                    k = tangent(dz[j], dy[j], dx[j], ez[j], ey[j], ex[j], b)
                    ring_g[s, :, block(j)] = turn(dy[j], b[1], ey[j], k)

    def divergence(fz, fxy, z, t, j):
        at = (pl.ds(8 * t, 8), block(j))
        return 0.25 * ((fz[(z + 2, *at)] - fz[(z, *at)]) + fxy[(z, *at)])

    def laplacian(buf, zc, lo, hi):
        c, below, above = layer(buf, zc), layer(buf, zc - 1), layer(buf, zc + 1)
        down, up = shift_y(c, lo, hi)
        out = blank()
        for t in range(T):
            l, h = shift_x(c[t])
            for j in range(C):
                total = (below[t][j] + above[t][j]) + (down[t][j] + up[t][j])
                out[t][j] = c[t][j] + TIME_STEP * (total + (l[j] + h[j]) - 6.0 * c[t][j])
        return out

    def reaction(p, u):
        x = DRIVE_SHARP * (MELT_POINT - u)
        m = DRIVE_SCALE / math.pi * arctan(x)
        well = p * (1.0 - p)
        tilt = p - 0.5 + m
        slope = (-DRIVE_SHARP * DRIVE_SCALE / math.pi) * recip(1.0 + x * x)
        return well * tilt, (1.0 - 2.0 * p) * tilt + well, well * slope

    def over(lo, hi, body, unroll=4):
        if hi - lo <= unroll:
            for z in range(lo, hi):
                body(z)
            return

        def some_layers(i, carry):
            for k in range(unroll):
                body(lo + i * unroll + k)
            return carry
        lax.fori_loop(0, (hi - lo) // unroll, some_layers, 0)
        for z in range(hi - (hi - lo) % unroll, hi):
            body(z)

    def inner(body):
        over(1, Z - 1, body, 3)

    def outer(body):
        body(0)
        body(Z - 1)

    def per_tile(body):
        def whole(z):
            for t in range(T):
                for j in range(C):
                    body(z, t, j)
        return whole

    def get(buf, z, t, j):
        return buf[z, pl.ds(8 * t, 8), block(j)]

    m_p0, m_y0, m_c0 = thick(p0), along_y(sy0, ry0), corners(sc0, rc0)
    m_u0, m_d1, m_t1 = thin(u0), thick(d1), thin(t1)
    m_y1, m_c1 = along_y(sy1, ry1), corners(sc1, rc1)
    m_p1, m_y2, m_c2 = thick(p1), along_y(sy2, ry2), corners(sc2, rc2)
    m_d0, m_t0 = thick(d0), thin(t0)
    m_y3, m_c3 = along_y(sy3, ry3), corners(sc3, rc3)

    @pl.when(zi == 0)
    def _():
        for buf in (p0, p1, d1, d0):
            buf[pl.ds(0, 2)] = jnp.zeros((2,) + buf.shape[1:], jnp.float32)
        for buf in (u0, t1, t0):
            buf[0] = jnp.zeros(buf.shape[1:], jnp.float32)

    @pl.when(zi == nz - 1)
    def _():
        for buf in (p0, p1, d1, d0):
            buf[pl.ds(Z + 2, 2)] = jnp.zeros((2,) + buf.shape[1:], jnp.float32)
        for buf in (u0, t1, t0):
            buf[Z + 1] = jnp.zeros(buf.shape[1:], jnp.float32)

    for s, at_end in ((0, yi == 0), (1, yi == ny - 1)):
        @pl.when(at_end)
        def _(s=s):
            for buf in (ry0, ry1, ry2, ry3):
                buf[s] = jnp.zeros(buf.shape[1:], jnp.float32)

    for i, side in enumerate(SIDES[4:]):
        @pl.when(jnp.logical_not(there(opposite(side))))
        def _(i=i):
            for buf in (rc0, rc1, rc2, rc3):
                buf[i] = jnp.zeros(buf.shape[1:], jnp.float32)

    def one(cond):
        return jnp.where(cond, 1, 0)

    local[0].wait()
    pack(p0, 2, 2, sy0, 0)
    pack_corner(p0, sc0)
    near_z = one(zi > 0) + one(zi < nz - 1)
    near_y = one(yi > 0) + one(yi < ny - 1)
    pl.semaphore_wait(barrier, near_z + near_y + near_z * near_y)
    start(m_y0 + m_c0 + m_p0)

    for copy in local[1:]:
        copy.wait()

    @per_tile
    def weight(z, t, j):
        w = get(sb, z, t, j) + LATENT_HEAT * get(t1, z + 1, t, j)
        store(d1, z + 2, t, j, TIME_STEP * get(kb, z, t, j) * w)
    over(0, Z, weight)
    pack(u0, 1, 1, sy1, 0)
    pack(d1, 2, 2, sy1, 1)
    pack(t1, 1, 1, sy1, 3)
    pack_corner(d1, sc1)
    start(m_y1 + m_c1 + m_u0 + m_d1 + m_t1)

    @per_tile
    def first_terms(z, t, j):
        a, b, c = reaction(get(p0, z + 2, t, j), get(u0, z + 1, t, j))
        store(r0, z, t, j, a)
        store(rp0, z, t, j, b)
        store(ru0, z, t, j, c)
    over(0, Z, first_terms)

    arrive(m_y0 + m_c0)
    flux_ring((ry0, 0, sy0, 0, rc0, 0))

    def flux0(z):
        flux_layer(p0, z + 2, halo_rows(ry0, 0, z), ring=z)
    inner(flux0)
    arrive(m_p0)
    outer(flux0)
    flux_layer(p0, 1, corner_rows(rc0, 0, True))
    flux_layer(p0, Z + 2, corner_rows(rc0, 0, False))

    @per_tile
    def advance(z, t, j):
        growth = divergence(jz, jxy, z, t, j) + get(r0, z, t, j)
        store(gr0, z, t, j, growth)
        gain = TIME_STEP * get(kb, z, t, j) * growth
        store(p1, z + 2, t, j, get(p0, z + 2, t, j) + gain)
    for z in (0, 1, Z - 2, Z - 1):
        advance(z)
    pack_corner(p1, sc2)
    start(m_c2 + m_p1)
    over(2, Z - 2, advance)
    pack(p1, 2, 2, sy2, 0)
    start(m_y2)

    arrive(m_y1 + m_c1 + m_u0 + m_d1 + m_t1)

    def second_terms(z):
        new_u = laplacian(u0, z + 1, *halo_rows(ry1, 0, z))
        new_t = laplacian(t1, z + 1, *halo_rows(ry1, 3, z))
        for t in range(T):
            for j in range(C):
                p = get(p1, z + 2, t, j)
                u = new_u[t][j] + LATENT_HEAT * (p - get(p0, z + 2, t, j))
                a, b, c = reaction(p, u)
                store(r1, z, t, j, a)
                store(rp1, z, t, j, b)
                store(ru1, z, t, j, c)
                store(tl1, z, t, j, new_t[t][j])
    over(0, Z, second_terms, 2)

    arrive(m_y2 + m_c2)
    flux_ring((ry2, 0, sy2, 0, rc2, 0), (ry1, 1, sy1, 1, rc1, 0))

    def adjoint1(z):
        flux_layer(p1, z + 2, halo_rows(ry2, 0, z), d1, halo_rows(ry1, 1, z), ring=z)
    inner(adjoint1)
    arrive(m_p1)
    outer(adjoint1)
    flux_layer(p1, 1, corner_rows(rc2, 0, True), d1, corner_rows(rc1, 0, True))
    flux_layer(p1, Z + 2, corner_rows(rc2, 0, False), d1, corner_rows(rc1, 0, False))

    @per_tile
    def middle(z, t, j):
        d = get(d1, z + 2, t, j)
        pb = get(sb, z, t, j) + d * get(rp1, z, t, j) + divergence(gz, gxy, z, t, j)
        ub = get(tl1, z, t, j) + d * get(ru1, z, t, j)
        store(pb0, z, t, j, pb)
        store(t0, z + 1, t, j, ub)
        store(d0, z + 2, t, j, TIME_STEP * get(kb, z, t, j) * (pb + LATENT_HEAT * ub))
    for z in (0, 1, Z - 2, Z - 1):
        middle(z)
    pack_corner(d0, sc3)
    start(m_c3 + m_d0 + m_t0)
    over(2, Z - 2, middle)
    pack(d0, 2, 2, sy3, 0)
    pack(t0, 1, 1, sy3, 2)
    start(m_y3)

    @per_tile
    def mobility(z, t, j):
        growth = divergence(jz, jxy, z, t, j) + get(r1, z, t, j)
        late = get(sb, z, t, j) + LATENT_HEAT * get(t1, z + 1, t, j)
        early = get(pb0, z, t, j) + LATENT_HEAT * get(t0, z + 1, t, j)
        store(gm_out, z, t, j, TIME_STEP * (late * growth + early * get(gr0, z, t, j)))
    over(0, Z, mobility)
    writes = [pltpu.make_async_copy(gm_out, gm_hbm, lsem.at[5])]
    writes[0].start()

    arrive(m_y3 + m_c3)
    flux_ring((ry0, 0, sy0, 0, rc0, 0), (ry3, 0, sy3, 0, rc3, 0), False)

    def adjoint0(z):
        flux_layer(p0, z + 2, halo_rows(ry0, 0, z), d0, halo_rows(ry3, 0, z), False, ring=z)
    inner(adjoint0)
    arrive(m_d0 + m_t0)
    outer(adjoint0)
    flux_layer(p0, 1, corner_rows(rc0, 0, True), d0, corner_rows(rc3, 0, True), False)
    flux_layer(p0, Z + 2, corner_rows(rc0, 0, False), d0, corner_rows(rc3, 0, False), False)

    def finish(z):
        new_t = laplacian(t0, z + 1, *halo_rows(ry3, 2, z))
        for t in range(T):
            for j in range(C):
                d = get(d0, z + 2, t, j)
                pb = get(pb0, z, t, j) + d * get(rp0, z, t, j)
                store(sp_out, z, t, j, pb + divergence(gz, gxy, z, t, j))
                store(st_out, z, t, j, new_t[t][j] + d * get(ru0, z, t, j))
    half = Z // 2
    for i in (0, 1):
        over(i * half, (i + 1) * half, finish, 2)
        part = pl.ds(i * half, half)
        for k, (src, dst) in enumerate(((sp_out, sp_hbm), (st_out, st_hbm))):
            writes.append(pltpu.make_async_copy(src.at[part], dst.at[part], lsem.at[6 + 2 * i + k]))
            writes[-1].start()

    sent(m_p0 + m_y0 + m_c0 + m_u0 + m_d1 + m_t1 + m_y1 + m_c1)
    sent(m_p1 + m_y2 + m_c2 + m_d0 + m_t0 + m_y3 + m_c3)
    for copy in writes:
        copy.wait()


def body(nz, ny, *blocks):
    Z, Y, X = blocks[0].shape

    def buf(*shape):
        return pltpu.VMEM(shape, jnp.float32)

    thick, thin, flat = (Z + 4, Y, X), (Z + 2, Y, X), (Z, Y, X)
    scratch = [buf(*flat)] * 3 + [buf(*thick)] * 4 + [buf(*thin)] * 3 + [buf(*flat)] * 3
    scratch += [buf(*thin), buf(*flat)] * 2
    scratch += [buf(*flat)] * 9
    scratch += [buf(2, Z, X)] * 2
    scratch += [buf(2, n, Z, X) for n in (2, 2, 4, 4, 2, 2, 3, 3)]
    scratch += [buf(4, 1, 1, X)] * 8
    count = 38
    scratch += [pltpu.SemaphoreType.DMA((count,))] * 2 + [pltpu.SemaphoreType.DMA((10,))]
    hbm = pl.BlockSpec(memory_space=pltpu.HBM)
    out = jax.ShapeDtypeStruct((Z, Y, X), jnp.float32)
    return pl.pallas_call(
        functools.partial(kernel, nz, ny),
        out_shape=(out, out, out),
        in_specs=[hbm] * 5,
        out_specs=(hbm, hbm, hbm),
        scratch_shapes=scratch,
        compiler_params=pltpu.CompilerParams(
            collective_id=0, has_side_effects=True, vmem_limit_bytes=62 * 1024 * 1024
        ),
    )(*blocks)


def solution(mesh):
    spec = P("gz", "gy", None)
    return jax.shard_map(
        functools.partial(body, mesh.shape["gz"], mesh.shape["gy"]),
        mesh=mesh,
        in_specs=(spec,) * 5,
        out_specs=(spec,) * 3,
        check_vma=False,
    )
```

```python
import functools
import math

import jax
import jax.numpy as jnp
from jax import lax
from jax.experimental import pallas as pl
from jax.experimental.pallas import tpu as pltpu
from jax.sharding import PartitionSpec as P

TIME_STEP = 0.15
ANISOTROPY = 0.05
GRAD_FLOOR = 0.01
LATENT_HEAT = 1.8
DRIVE_SCALE = 0.9
DRIVE_SHARP = 10.0
MELT_POINT = 1.0

BASE = 1.0 - 3.0 * ANISOTROPY
RISE = 4.0 * ANISOTROPY
HALF_BASE = 0.5 * BASE
FALL = 8.0 * ANISOTROPY - 0.5 * RISE
TWIST = 8.0 * ANISOTROPY
SLOPE_0 = RISE * HALF_BASE - FALL * BASE
SLOPE_1 = -2.0 * RISE * FALL
FLOOR = 4.0 * GRAD_FLOOR

ATAN = (
    1.0, -0.3333328366279602, 0.19998230040073395, -0.14261573553085327,
    0.10940198600292206, -0.08372063934803009, 0.05746355652809143,
    -0.030717508867383003, 0.010680719278752804, -0.0017437011701986194,
)

SIDES = ((1, 0), (-1, 0), (0, 1), (0, -1), (1, 1), (1, -1), (-1, 1), (-1, -1))


def recip(x):
    r = pl.reciprocal(x, approx=True)
    return r * (2.0 - x * r)


def arctan(x):
    size = jnp.abs(x)
    big = size > 1.0
    y = jnp.where(big, recip(jnp.maximum(size, 1.0)), size)
    z = y * y
    total = jnp.full_like(z, ATAN[-1])
    for c in ATAN[-2::-1]:
        total = total * z + c
    total = total * y
    total = jnp.where(big, 0.5 * math.pi - total, total)
    return jnp.where(x < 0.0, -total, total)


def basis(dz, dy, dx):
    zz, yy, xx = dz * dz, dy * dy, dx * dx
    s = zz + yy + xx + FLOOR
    r = recip(s)
    qs = (zz * zz + yy * yy + xx * xx) * r
    q = qs * r
    a = BASE + RISE * q
    big_a = a * (HALF_BASE - FALL * q)
    big_b = TWIST * a * r
    return zz, yy, xx, r, qs, q, a, big_a, big_b


def flux_of(d, sq, b):
    return d * (b[7] + b[8] * sq)


def tangent(dz, dy, dx, ez, ey, ex, b):
    zz, yy, xx, r, qs, q, a, big_a, big_b = b
    mz, my, mx = dz * ez, dy * ey, dx * ex
    g = mz + my + mx
    t = zz * mz + yy * my + xx * mx
    dq = (4.0 * r * r) * (t - qs * g)
    d_a = (SLOPE_0 + SLOPE_1 * q) * dq
    d_b = r * (TWIST * RISE * dq - (2.0 * TWIST) * a * r * g)
    return big_a, 3.0 * big_b, d_a, d_b


def turn(d, sq, e, t):
    return (t[0] + t[1] * sq) * e + d * (t[2] + t[3] * sq)


def kernel(
    nz, ny,
    p_in, u_in, k_in, ps_in, ts_in,
    sp_hbm, st_hbm, gm_hbm,
    sp_out, st_out, gm_out,
    p0, p1, d1, d0, u0, t1, t0, u1, kb, sb,
    jz, jxy, gz, gxy,
    r0, rp0, ru0, r1, rp1, ru1, tl1, gr0, pb0,
    ring_j, ring_g,
    sy0, ry0, sy1, ry1, sy2, ry2, sy3, ry3,
    sc0, rc0, sc1, rc1, sc2, rc2, sc3, rc3,
    ssem, rsem, lsem,
):
    Z, Y, X = p_in.shape
    T, C = Y // 8, X // 128
    zi, yi = lax.axis_index("gz"), lax.axis_index("gy")

    def there(side):
        cond = None
        for step, at, count in ((side[0], zi, nz), (side[1], yi, ny)):
            if step:
                c = at < count - 1 if step > 0 else at > 0
                cond = c if cond is None else jnp.logical_and(cond, c)
        return cond

    def opposite(side):
        return (-side[0], -side[1])

    barrier = pltpu.get_barrier_semaphore()
    for side in SIDES:
        @pl.when(there(side))
        def _(side=side):
            pl.semaphore_signal(
                barrier, inc=1, device_id=(zi + side[0], yi + side[1]),
                device_id_type=pl.DeviceIdType.MESH,
            )

    local = [
        pltpu.make_async_copy(src, dst, lsem.at[i])
        for i, (src, dst) in enumerate((
            (ps_in, sb),
            (ts_in, t1.at[pl.ds(1, Z)]),
            (k_in, kb),
            (p_in, p0.at[pl.ds(2, Z)]),
            (u_in, u0.at[pl.ds(1, Z)]),
            (p_in.at[:, 0], sy0.at[0, 0]),
            (p_in.at[:, Y - 1], sy0.at[1, 0]),
        ))
    ]
    for copy in local:
        copy.start()

    slots = iter(range(rsem.shape[0]))

    def message(side, src, dst):
        slot = next(slots)
        copy = pltpu.make_async_remote_copy(
            src_ref=src, dst_ref=dst, send_sem=ssem.at[slot], recv_sem=rsem.at[slot],
            device_id=(zi + side[0], yi + side[1]), device_id_type=pl.DeviceIdType.MESH,
        )
        return side, copy

    def start(messages):
        for side, copy in messages:
            pl.when(there(side))(copy.start)

    def arrive(messages):
        for side, copy in messages:
            pl.when(there(opposite(side)))(copy.wait_recv)

    def sent(messages):
        for side, copy in messages:
            pl.when(there(side))(copy.wait_send)

    def thick(buf):
        return [
            message((1, 0), buf.at[pl.ds(Z, 2)], buf.at[pl.ds(0, 2)]),
            message((-1, 0), buf.at[pl.ds(2, 2)], buf.at[pl.ds(Z + 2, 2)]),
        ]

    def thin(buf):
        return [
            message((1, 0), buf.at[pl.ds(Z, 1)], buf.at[pl.ds(0, 1)]),
            message((-1, 0), buf.at[pl.ds(1, 1)], buf.at[pl.ds(Z + 1, 1)]),
        ]

    def along_y(src, dst, at, deep=1):
        part = pl.ds(at, deep)
        return [
            message((0, 1), src.at[1, part], dst.at[0, part]),
            message((0, -1), src.at[0, part], dst.at[1, part]),
        ]

    def thick_in(src, buf):
        return [
            message((1, 0), src.at[pl.ds(Z - 2, 2)], buf.at[pl.ds(0, 2)]),
            message((-1, 0), src.at[pl.ds(0, 2)], buf.at[pl.ds(Z + 2, 2)]),
        ]

    def thin_in(src, buf):
        return [
            message((1, 0), src.at[pl.ds(Z - 1, 1)], buf.at[pl.ds(0, 1)]),
            message((-1, 0), src.at[pl.ds(0, 1)], buf.at[pl.ds(Z + 1, 1)]),
        ]

    def row_in(src, y, dst, at):
        return [
            message((0, 1), src.at[:, Y - 1 - y], dst.at[0, at]),
            message((0, -1), src.at[:, y], dst.at[1, at]),
        ]

    def corners_in(src, dst):
        return [
            message(
                side, src.at[Z - 1 if side[0] > 0 else 0, Y - 1 if side[1] > 0 else 0],
                dst.at[i, 0, 0],
            )
            for i, side in enumerate(SIDES[4:])
        ]

    def corners(src, dst):
        return [message(side, src.at[i], dst.at[i]) for i, side in enumerate(SIDES[4:])]

    lane = lax.broadcasted_iota(jnp.int32, (8, 128), 1)
    row = lax.broadcasted_iota(jnp.int32, (8, 128), 0)
    top, bottom = row == 0, row == 7
    first, last = lane == 0, lane == 127

    def block(j):
        return pl.ds(128 * j, 128)

    def layer(buf, z):
        return [[buf[z, pl.ds(8 * t, 8), block(j)] for j in range(C)] for t in range(T)]

    def store(buf, z, t, j, value):
        buf[z, pl.ds(8 * t, 8), block(j)] = value

    def wide_row(buf, *at):
        return [
            jnp.broadcast_to(buf[(*at[:-1], pl.ds(at[-1], 1), block(j))], (8, 128))
            for j in range(C)
        ]

    def shift_x(row_of_tiles, end=None):
        before = [pltpu.roll(c, 1, 1) for c in row_of_tiles]
        after = [pltpu.roll(c, 127, 1) for c in row_of_tiles]
        zero = 0.0
        lo = [
            jnp.where(first, before[j - 1] if j else (zero if end is None else end), before[j])
            for j in range(C)
        ]
        hi = [
            jnp.where(
                last, after[j + 1] if j < C - 1 else (zero if end is None else -end), after[j]
            )
            for j in range(C)
        ]
        return lo, hi

    def shift_y(tiles, lo, hi):
        before = [[pltpu.roll(c, 1, 0) for c in r] for r in tiles]
        after = [[pltpu.roll(c, 7, 0) for c in r] for r in tiles]
        down = [
            [jnp.where(top, before[t - 1][j] if t else lo[j], before[t][j]) for j in range(C)]
            for t in range(T)
        ]
        up = [
            [jnp.where(bottom, after[t + 1][j] if t < T - 1 else hi[j], after[t][j]) for j in range(C)]
            for t in range(T)
        ]
        return down, up

    def sub(a, b):
        if isinstance(a, list):
            return [sub(x, y) for x, y in zip(a, b)]
        return a - b

    def diffs(buf, zc, lo, hi):
        c = layer(buf, zc)
        dz = sub(layer(buf, zc + 1), layer(buf, zc - 1))
        down, up = shift_y(c, lo, hi)
        sides = [shift_x(r) for r in c]
        return c, dz, sub(up, down), [sub(h, l) for l, h in sides]

    def halo_rows(rim, at, z):
        at = () if at is None else (at,)
        if isinstance(z, int):
            return wide_row(rim, 0, *at, z), wide_row(rim, 1, *at, z)
        down = lax.rem(Z - z, 8)
        lo = [pltpu.roll(rim[(0, *at, slice(None), block(j))], down, 0) for j in range(C)]
        hi = [pltpu.roll(rim[(1, *at, slice(None), block(j))], 7 - z, 0) for j in range(C)]
        return lo, hi

    def corner_rows(corner, at, below):
        sz = 1 if below else -1
        lo = SIDES[4:].index((sz, 1))
        hi = SIDES[4:].index((sz, -1))
        return wide_row(corner, lo, at, 0), wide_row(corner, hi, at, 0)

    def ring_diffs(rim, at, edge, edge_at, corner, corner_at, s):
        near = [rim[s, at, :, block(j)] for j in range(C)]
        far = [rim[s, at + 1, :, block(j)] for j in range(C)]
        mine = [edge[s, edge_at, :, block(j)] for j in range(C)]
        sy = 1 if s == 0 else -1
        lo = wide_row(corner, SIDES[4:].index((1, sy)), corner_at, 0)
        hi = wide_row(corner, SIDES[4:].index((-1, sy)), corner_at, 0)
        (dn,), (up,) = ring_shift(near, lo, hi)
        l, h = shift_x(near)
        dy = sub(mine, far) if s == 0 else sub(far, mine)
        return sub(up, dn), dy, sub(h, l)

    def ring_shift(near, lo, hi):
        down = [jnp.where(top, lo[j], pltpu.roll(near[j], 1, 0)) for j in range(C)]
        up = [jnp.where(bottom, hi[j], pltpu.roll(near[j], 7, 0)) for j in range(C)]
        return [down], [up]

    def pack(src, base, deep, dst, at, skip=0):
        for k in range(skip, deep):
            for s, y in ((0, k), (1, Y - 1 - k)):
                total = wide_row(src, base, y)
                for z in range(1, Z):
                    now = wide_row(src, base + z, y)
                    total = [jnp.where(row == z, n, o) for n, o in zip(now, total)]
                for j in range(C):
                    dst[s, at + k, :, block(j)] = total[j]

    def pack_corner(src, dst):
        for i, (sz, sy) in enumerate(SIDES[4:]):
            zc = Z + 1 if sz > 0 else 2
            yc = Y - 1 if sy > 0 else 0
            dst[i, 0] = src[zc, pl.ds(yc, 1), :]

    def ends(tiles):
        return jnp.where(first, tiles[0], jnp.where(last, tiles[C - 1], 0.0))

    def end_basis(d):
        xx = d * d
        r = recip(xx + FLOOR)
        qs = xx * xx * r
        q = qs * r
        a = BASE + RISE * q
        return d, xx, r, qs, q, a, a * (HALF_BASE - FALL * q), TWIST * a * r

    def end_flux(b):
        d, xx, r, qs, q, a, big_a, big_b = b
        return d * (big_a + big_b * xx)

    def end_tangent(b, e):
        d, xx, r, qs, q, a, big_a, big_b = b
        m = d * e
        dq = (4.0 * r * r) * (xx * m - qs * m)
        d_a = (SLOPE_0 + SLOPE_1 * q) * dq
        d_b = r * (TWIST * RISE * dq - (2.0 * TWIST) * a * r * m)
        return (big_a + 3.0 * big_b * xx) * e + d * (d_a + d_b * xx)

    def cross(fx, fy, end):
        out = []
        down, up = shift_y(fy, [0.0] * C, [0.0] * C)
        for t in range(T):
            l, h = shift_x(fx[t], end[t])
            out.append([(h[j] - l[j]) + (up[t][j] - down[t][j]) for j in range(C)])
        return out

    def blank():
        return [[None] * C for _ in range(T)]

    def flux_layer(p, zc, p_rows, d=None, d_rows=None, with_flux=True, ring=None):
        c, dz, dy, dx = diffs(p, zc, *p_rows)
        if d is not None:
            e, ez, ey, ex = diffs(d, zc, *d_rows)
        fx, fy, hx, hy = blank(), blank(), blank(), blank()
        for t in range(T):
            for j in range(C):
                a = (dz[t][j], dy[t][j], dx[t][j])
                b = basis(*a)
                if with_flux:
                    store(jz, zc - 1, t, j, flux_of(a[0], b[0], b))
                    if ring is not None:
                        fy[t][j] = flux_of(a[1], b[1], b)
                        fx[t][j] = flux_of(a[2], b[2], b)
                if d is not None:
                    v = (ez[t][j], ey[t][j], ex[t][j])
                    k = tangent(*a, *v, b)
                    store(gz, zc - 1, t, j, turn(a[0], b[0], v[0], k))
                    if ring is not None:
                        hy[t][j] = turn(a[1], b[1], v[1], k)
                        hx[t][j] = turn(a[2], b[2], v[2], k)
        if ring is None:
            return
        eb = [end_basis(ends(r)) for r in c]
        if with_flux:
            out = cross(fx, fy, [end_flux(b) for b in eb])
            for t in range(T):
                for j in range(C):
                    store(jxy, ring, t, j, out[t][j])
        if d is not None:
            out = cross(hx, hy, [end_tangent(b, ends(r)) for b, r in zip(eb, e)])
            for t in range(T):
                for j in range(C):
                    store(gxy, ring, t, j, out[t][j])

    def flux_ring(p_args, d_args=None, with_flux=True):
        for s in (0, 1):
            dz, dy, dx = ring_diffs(*p_args, s)
            if d_args is not None:
                ez, ey, ex = ring_diffs(*d_args, s)
            for j in range(C):
                b = basis(dz[j], dy[j], dx[j])
                if with_flux:
                    ring_j[s, :, block(j)] = flux_of(dy[j], b[1], b)
                if d_args is not None:
                    k = tangent(dz[j], dy[j], dx[j], ez[j], ey[j], ex[j], b)
                    ring_g[s, :, block(j)] = turn(dy[j], b[1], ey[j], k)

    def divergence(fz, fxy, ring, z):
        lo, hi = halo_rows(ring, None, z)
        out = blank()
        for t in range(T):
            for j in range(C):
                at = (pl.ds(8 * t, 8), block(j))
                total = (fz[(z + 2, *at)] - fz[(z, *at)]) + fxy[(z, *at)]
                if t == 0:
                    total = jnp.where(top, total - lo[j], total)
                if t == T - 1:
                    total = jnp.where(bottom, total + hi[j], total)
                out[t][j] = 0.25 * total
        return out

    def laplacian(buf, zc, lo, hi):
        c, below, above = layer(buf, zc), layer(buf, zc - 1), layer(buf, zc + 1)
        down, up = shift_y(c, lo, hi)
        out = blank()
        for t in range(T):
            l, h = shift_x(c[t])
            for j in range(C):
                total = (below[t][j] + above[t][j]) + (down[t][j] + up[t][j])
                out[t][j] = c[t][j] + TIME_STEP * (total + (l[j] + h[j]) - 6.0 * c[t][j])
        return out

    def reaction(p, u):
        x = DRIVE_SHARP * (MELT_POINT - u)
        m = DRIVE_SCALE / math.pi * arctan(x)
        well = p * (1.0 - p)
        tilt = p - 0.5 + m
        slope = (-DRIVE_SHARP * DRIVE_SCALE / math.pi) * recip(1.0 + x * x)
        return well * tilt, (1.0 - 2.0 * p) * tilt + well, well * slope

    def over(lo, hi, body, unroll=4):
        if hi - lo <= unroll:
            for z in range(lo, hi):
                body(z)
            return

        def some_layers(i, carry):
            for k in range(unroll):
                body(lo + i * unroll + k)
            return carry
        lax.fori_loop(0, (hi - lo) // unroll, some_layers, 0)
        for z in range(hi - (hi - lo) % unroll, hi):
            body(z)

    def inner(body):
        over(1, Z - 1, body, 3)

    def outer(body):
        body(0)
        body(Z - 1)

    def per_tile(body):
        def whole(z):
            for t in range(T):
                for j in range(C):
                    body(z, t, j)
        return whole

    def with_divergence(fz, fxy, ring, body):
        def whole(z):
            div = divergence(fz, fxy, ring, z)
            for t in range(T):
                for j in range(C):
                    body(z, t, j, div[t][j])
        return whole

    def get(buf, z, t, j):
        return buf[z, pl.ds(8 * t, 8), block(j)]

    m_y0, m_p0 = row_in(p_in, 0, ry0, 0), thick_in(p_in, p0)
    m_f0, m_c0 = row_in(p_in, 1, ry0, 1), corners_in(p_in, rc0)
    m_d1, m_y1, m_c1 = thick(d1), along_y(sy1, ry1, 1, 2), corners(sc1, rc1)
    m_ut = thin_in(u_in, u0) + thin_in(ts_in, t1)
    m_ut += row_in(u_in, 0, ry1, 0) + row_in(ts_in, 0, ry1, 3)
    m_y2, m_p1 = along_y(sy2, ry2, 0), thick(p1)
    m_f2, m_c2 = along_y(sy2, ry2, 1), corners(sc2, rc2)
    m_y3, m_d0, m_t0 = along_y(sy3, ry3, 0), thick(d0), thin(t0)
    m_f3, m_c3 = along_y(sy3, ry3, 1, 2), corners(sc3, rc3)

    @pl.when(zi == 0)
    def _():
        for buf in (p0, p1, d1, d0):
            buf[pl.ds(0, 2)] = jnp.zeros((2,) + buf.shape[1:], jnp.float32)
        for buf in (u0, t1, t0):
            buf[0] = jnp.zeros(buf.shape[1:], jnp.float32)

    @pl.when(zi == nz - 1)
    def _():
        for buf in (p0, p1, d1, d0):
            buf[pl.ds(Z + 2, 2)] = jnp.zeros((2,) + buf.shape[1:], jnp.float32)
        for buf in (u0, t1, t0):
            buf[Z + 1] = jnp.zeros(buf.shape[1:], jnp.float32)

    for s, at_end in ((0, yi == 0), (1, yi == ny - 1)):
        @pl.when(at_end)
        def _(s=s):
            for buf in (ry0, ry1, ry2, ry3):
                buf[s] = jnp.zeros(buf.shape[1:], jnp.float32)

    for i, side in enumerate(SIDES[4:]):
        @pl.when(jnp.logical_not(there(opposite(side))))
        def _(i=i):
            for buf in (rc0, rc1, rc2, rc3):
                buf[i] = jnp.zeros(buf.shape[1:], jnp.float32)

    def one(cond):
        return jnp.where(cond, 1, 0)

    near_z = one(zi > 0) + one(zi < nz - 1)
    near_y = one(yi > 0) + one(yi < ny - 1)
    pl.semaphore_wait(barrier, near_z + near_y + near_z * near_y)
    start(m_y0 + m_p0 + m_f0 + m_c0)

    for copy in local[:3]:
        copy.wait()

    @per_tile
    def weight(z, t, j):
        w = get(sb, z, t, j) + LATENT_HEAT * get(t1, z + 1, t, j)
        store(d1, z + 2, t, j, TIME_STEP * get(kb, z, t, j) * w)
    over(0, Z, weight)
    pack(d1, 2, 2, sy1, 1)
    pack_corner(d1, sc1)
    start(m_d1 + m_y1 + m_c1 + m_ut)
    for copy in local[3:]:
        copy.wait()

    @per_tile
    def first_terms(z, t, j):
        a, b, c = reaction(get(p0, z + 2, t, j), get(u0, z + 1, t, j))
        store(r0, z, t, j, a)
        store(rp0, z, t, j, b)
        store(ru0, z, t, j, c)
    over(0, Z, first_terms)

    def flux0(z):
        flux_layer(p0, z + 2, halo_rows(ry0, 0, z), ring=z)
    arrive(m_y0)
    inner(flux0)
    arrive(m_f0 + m_c0)
    flux_ring((ry0, 0, sy0, 0, rc0, 0))
    arrive(m_p0)
    outer(flux0)
    flux_layer(p0, 1, corner_rows(rc0, 0, True))
    flux_layer(p0, Z + 2, corner_rows(rc0, 0, False))

    def advance_cell(z, t, j, div):
        growth = div + get(r0, z, t, j)
        store(gr0, z, t, j, growth)
        gain = TIME_STEP * get(kb, z, t, j) * growth
        store(p1, z + 2, t, j, get(p0, z + 2, t, j) + gain)
    advance = with_divergence(jz, jxy, ring_j, advance_cell)
    over(0, Z, advance)
    pack(p1, 2, 1, sy2, 0)
    start(m_y2 + m_p1)
    pack_corner(p1, sc2)
    start(m_c2)
    pack(p1, 2, 2, sy2, 0, 1)
    start(m_f2)

    arrive(m_ut)

    def second_terms(z):
        new_u = laplacian(u0, z + 1, *halo_rows(ry1, 0, z))
        new_t = laplacian(t1, z + 1, *halo_rows(ry1, 3, z))
        for t in range(T):
            for j in range(C):
                p = get(p1, z + 2, t, j)
                u = new_u[t][j] + LATENT_HEAT * (p - get(p0, z + 2, t, j))
                a, b, c = reaction(p, u)
                store(r1, z, t, j, a)
                store(rp1, z, t, j, b)
                store(ru1, z, t, j, c)
                store(tl1, z, t, j, new_t[t][j])
    over(0, Z, second_terms, 2)

    def adjoint1(z):
        flux_layer(p1, z + 2, halo_rows(ry2, 0, z), d1, halo_rows(ry1, 1, z), ring=z)
    arrive(m_y1 + m_c1 + m_d1 + m_y2)
    inner(adjoint1)
    arrive(m_f2 + m_c2)
    flux_ring((ry2, 0, sy2, 0, rc2, 0), (ry1, 1, sy1, 1, rc1, 0))
    arrive(m_p1)
    outer(adjoint1)
    flux_layer(p1, 1, corner_rows(rc2, 0, True), d1, corner_rows(rc1, 0, True))
    flux_layer(p1, Z + 2, corner_rows(rc2, 0, False), d1, corner_rows(rc1, 0, False))

    def middle_cell(z, t, j, div):
        d = get(d1, z + 2, t, j)
        pb = get(sb, z, t, j) + d * get(rp1, z, t, j) + div
        ub = get(tl1, z, t, j) + d * get(ru1, z, t, j)
        store(pb0, z, t, j, pb)
        store(t0, z + 1, t, j, ub)
        store(d0, z + 2, t, j, TIME_STEP * get(kb, z, t, j) * (pb + LATENT_HEAT * ub))
    middle = with_divergence(gz, gxy, ring_g, middle_cell)
    over(0, Z, middle)
    pack(d0, 2, 1, sy3, 0)
    start(m_y3 + m_d0)
    pack_corner(d0, sc3)
    start(m_c3)
    pack(d0, 2, 2, sy3, 0, 1)
    pack(t0, 1, 1, sy3, 2)
    start(m_f3 + m_t0)

    def mobility_cell(z, t, j, div):
        growth = div + get(r1, z, t, j)
        late = get(sb, z, t, j) + LATENT_HEAT * get(t1, z + 1, t, j)
        early = get(pb0, z, t, j) + LATENT_HEAT * get(t0, z + 1, t, j)
        store(gm_out, z, t, j, TIME_STEP * (late * growth + early * get(gr0, z, t, j)))
    mobility = with_divergence(jz, jxy, ring_j, mobility_cell)
    over(0, Z, mobility)
    writes = [pltpu.make_async_copy(gm_out, gm_hbm, lsem.at[7])]
    writes[0].start()

    def adjoint0(z):
        flux_layer(p0, z + 2, halo_rows(ry0, 0, z), d0, halo_rows(ry3, 0, z), False, ring=z)
    arrive(m_y3)
    inner(adjoint0)
    arrive(m_f3 + m_c3)
    flux_ring((ry0, 0, sy0, 0, rc0, 0), (ry3, 0, sy3, 0, rc3, 0), False)
    arrive(m_d0 + m_t0)
    outer(adjoint0)
    flux_layer(p0, 1, corner_rows(rc0, 0, True), d0, corner_rows(rc3, 0, True), False)
    flux_layer(p0, Z + 2, corner_rows(rc0, 0, False), d0, corner_rows(rc3, 0, False), False)

    def finish(z):
        new_t = laplacian(t0, z + 1, *halo_rows(ry3, 2, z))
        div = divergence(gz, gxy, ring_g, z)
        for t in range(T):
            for j in range(C):
                d = get(d0, z + 2, t, j)
                pb = get(pb0, z, t, j) + d * get(rp0, z, t, j)
                store(sp_out, z, t, j, pb + div[t][j])
                store(st_out, z, t, j, new_t[t][j] + d * get(ru0, z, t, j))
    half = Z // 2
    for i in (0, 1):
        over(i * half, (i + 1) * half, finish, 2)
        part = pl.ds(i * half, half)
        for k, (src, dst) in enumerate(((sp_out, sp_hbm), (st_out, st_hbm))):
            writes.append(pltpu.make_async_copy(src.at[part], dst.at[part], lsem.at[8 + 2 * i + k]))
            writes[-1].start()

    sent(m_y0 + m_p0 + m_f0 + m_c0 + m_d1 + m_y1 + m_c1 + m_ut)
    sent(m_y2 + m_p1 + m_f2 + m_c2 + m_y3 + m_d0 + m_t0 + m_f3 + m_c3)
    for copy in writes:
        copy.wait()


def deliver(*refs):
    ins, outs, sem = refs[:3], refs[3:6], refs[6]
    Z = ins[0].shape[0]
    copies = []
    for src, dst in zip(ins, outs):
        for z in range(0, Z, 2):
            part = pl.ds(z, 2)
            copies.append(pltpu.make_async_copy(src.at[part], dst.at[part], sem.at[len(copies)]))
            copies[-1].start()
    for copy in copies:
        copy.wait()


def body(nz, ny, *blocks):
    Z, Y, X = blocks[0].shape

    def buf(*shape):
        return pltpu.VMEM(shape, jnp.float32)

    thick, thin, flat = (Z + 4, Y, X), (Z + 2, Y, X), (Z, Y, X)
    scratch = [buf(*flat)] * 3 + [buf(*thick)] * 4 + [buf(*thin)] * 3 + [buf(*flat)] * 3
    scratch += [buf(*thin), buf(*flat)] * 2
    scratch += [buf(*flat)] * 9
    scratch += [buf(2, Z, X)] * 2
    scratch += [buf(2, n, Z, X) for n in (2, 2, 4, 4, 2, 2, 3, 3)]
    scratch += [buf(4, 1, 1, X)] * 8
    count = 48
    scratch += [pltpu.SemaphoreType.DMA((count,))] * 2 + [pltpu.SemaphoreType.DMA((12,))]
    hbm = pl.BlockSpec(memory_space=pltpu.HBM)
    out = jax.ShapeDtypeStruct((Z, Y, X), jnp.float32)
    results = pl.pallas_call(
        functools.partial(kernel, nz, ny),
        out_shape=(out, out, out),
        in_specs=[hbm] * 5,
        out_specs=(hbm, hbm, hbm),
        scratch_shapes=scratch,
        compiler_params=pltpu.CompilerParams(
            collective_id=0, has_side_effects=True, vmem_limit_bytes=62 * 1024 * 1024
        ),
    )(*blocks)
    return pl.pallas_call(
        deliver,
        out_shape=(out, out, out),
        in_specs=[hbm] * 3,
        out_specs=(hbm, hbm, hbm),
        scratch_shapes=[pltpu.SemaphoreType.DMA((3 * (Z // 2),))],
        compiler_params=pltpu.CompilerParams(vmem_limit_bytes=62 * 1024 * 1024),
    )(*results)


def solution(mesh):
    spec = P("gz", "gy", None)
    return jax.shard_map(
        functools.partial(body, mesh.shape["gz"], mesh.shape["gy"]),
        mesh=mesh,
        in_specs=(spec,) * 5,
        out_specs=(spec,) * 3,
        check_vma=False,
    )
```

```python
import functools
import math

import jax
import jax.numpy as jnp
from jax import lax
from jax.experimental import pallas as pl
from jax.experimental.pallas import tpu as pltpu
from jax.sharding import PartitionSpec as P

TIME_STEP = 0.15
ANISOTROPY = 0.05
GRAD_FLOOR = 0.01
LATENT_HEAT = 1.8
DRIVE_SCALE = 0.9
DRIVE_SHARP = 10.0
MELT_POINT = 1.0

BASE = 1.0 - 3.0 * ANISOTROPY
RISE = 4.0 * ANISOTROPY
HALF_BASE = 0.5 * BASE
FALL = 8.0 * ANISOTROPY - 0.5 * RISE
TWIST = 8.0 * ANISOTROPY
SLOPE_0 = RISE * HALF_BASE - FALL * BASE
SLOPE_1 = -2.0 * RISE * FALL
FLOOR = 4.0 * GRAD_FLOOR

ATAN = (
    1.0, -0.3333328366279602, 0.19998230040073395, -0.14261573553085327,
    0.10940198600292206, -0.08372063934803009, 0.05746355652809143,
    -0.030717508867383003, 0.010680719278752804, -0.0017437011701986194,
)

SIDES = ((1, 0), (-1, 0), (0, 1), (0, -1), (1, 1), (1, -1), (-1, 1), (-1, -1))


def recip(x):
    r = pl.reciprocal(x, approx=True)
    return r * (2.0 - x * r)


def arctan(x):
    size = jnp.abs(x)
    big = size > 1.0
    y = jnp.where(big, recip(jnp.maximum(size, 1.0)), size)
    z = y * y
    total = jnp.full_like(z, ATAN[-1])
    for c in ATAN[-2::-1]:
        total = total * z + c
    total = total * y
    total = jnp.where(big, 0.5 * math.pi - total, total)
    return jnp.where(x < 0.0, -total, total)


def basis(dz, dy, dx):
    zz, yy, xx = dz * dz, dy * dy, dx * dx
    s = zz + yy + xx + FLOOR
    r = recip(s)
    qs = (zz * zz + yy * yy + xx * xx) * r
    q = qs * r
    a = BASE + RISE * q
    big_a = a * (HALF_BASE - FALL * q)
    big_b = TWIST * a * r
    return zz, yy, xx, r, qs, q, a, big_a, big_b


def flux_of(d, sq, b):
    return d * (b[7] + b[8] * sq)


def tangent(dz, dy, dx, ez, ey, ex, b):
    zz, yy, xx, r, qs, q, a, big_a, big_b = b
    mz, my, mx = dz * ez, dy * ey, dx * ex
    g = mz + my + mx
    t = zz * mz + yy * my + xx * mx
    dq = (4.0 * r * r) * (t - qs * g)
    d_a = (SLOPE_0 + SLOPE_1 * q) * dq
    d_b = r * (TWIST * RISE * dq - (2.0 * TWIST) * a * r * g)
    return big_a, 3.0 * big_b, d_a, d_b


def turn(d, sq, e, t):
    return (t[0] + t[1] * sq) * e + d * (t[2] + t[3] * sq)


def kernel(
    nz, ny,
    p_in, u_in, k_in, ps_in, ts_in,
    sp_out, st_out, gm_out,
    p0, p1, d1, d0, u0, t1, t0, u1, kb, sb,
    jz, jxy, gz, gxy,
    r0, rp0, ru0, r1, rp1, ru1, tl1, gr0, pb0,
    ring_j, ring_g,
    sy0, ry0, sy1, ry1, sy2, ry2, sy3, ry3,
    sc0, rc0, sc1, rc1, sc2, rc2, sc3, rc3,
    ssem, rsem, lsem,
):
    Z, Y, X = p_in.shape
    T, C = Y // 8, X // 128
    zi, yi = lax.axis_index("gz"), lax.axis_index("gy")

    def there(side):
        cond = None
        for step, at, count in ((side[0], zi, nz), (side[1], yi, ny)):
            if step:
                c = at < count - 1 if step > 0 else at > 0
                cond = c if cond is None else jnp.logical_and(cond, c)
        return cond

    def opposite(side):
        return (-side[0], -side[1])

    barrier = pltpu.get_barrier_semaphore()
    for side in SIDES:
        @pl.when(there(side))
        def _(side=side):
            pl.semaphore_signal(
                barrier, inc=1, device_id=(zi + side[0], yi + side[1]),
                device_id_type=pl.DeviceIdType.MESH,
            )

    local = [
        pltpu.make_async_copy(src, dst, lsem.at[i])
        for i, (src, dst) in enumerate(
            [
                (src.at[pl.ds(z, Z // 2)], dst.at[pl.ds(base + z, Z // 2)])
                for src, dst, base in (
                    (ps_in, sb, 0), (ts_in, t1, 1), (k_in, kb, 0), (p_in, p0, 2), (u_in, u0, 1)
                )
                for z in (0, Z // 2)
            ]
            + [(p_in.at[:, 0], sy0.at[0, 0]), (p_in.at[:, Y - 1], sy0.at[1, 0])]
        )
    ]
    for copy in local:
        copy.start()

    slots = iter(range(rsem.shape[0]))

    def message(side, src, dst):
        slot = next(slots)
        copy = pltpu.make_async_remote_copy(
            src_ref=src, dst_ref=dst, send_sem=ssem.at[slot], recv_sem=rsem.at[slot],
            device_id=(zi + side[0], yi + side[1]), device_id_type=pl.DeviceIdType.MESH,
        )
        return side, copy

    def start(messages):
        for side, copy in messages:
            pl.when(there(side))(copy.start)

    def arrive(messages):
        for side, copy in messages:
            pl.when(there(opposite(side)))(copy.wait_recv)

    def sent(messages):
        for side, copy in messages:
            pl.when(there(side))(copy.wait_send)

    def thick(buf):
        return [
            message((1, 0), buf.at[pl.ds(Z, 2)], buf.at[pl.ds(0, 2)]),
            message((-1, 0), buf.at[pl.ds(2, 2)], buf.at[pl.ds(Z + 2, 2)]),
        ]

    def thin(buf):
        return [
            message((1, 0), buf.at[pl.ds(Z, 1)], buf.at[pl.ds(0, 1)]),
            message((-1, 0), buf.at[pl.ds(1, 1)], buf.at[pl.ds(Z + 1, 1)]),
        ]

    def along_y(src, dst, at, deep=1):
        part = pl.ds(at, deep)
        return [
            message((0, 1), src.at[1, part], dst.at[0, part]),
            message((0, -1), src.at[0, part], dst.at[1, part]),
        ]

    def thick_in(src, buf):
        return [
            message((1, 0), src.at[pl.ds(Z - 2, 2)], buf.at[pl.ds(0, 2)]),
            message((-1, 0), src.at[pl.ds(0, 2)], buf.at[pl.ds(Z + 2, 2)]),
        ]

    def thin_in(src, buf):
        return [
            message((1, 0), src.at[pl.ds(Z - 1, 1)], buf.at[pl.ds(0, 1)]),
            message((-1, 0), src.at[pl.ds(0, 1)], buf.at[pl.ds(Z + 1, 1)]),
        ]

    def row_in(src, y, dst, at):
        return [
            message((0, 1), src.at[:, Y - 1 - y], dst.at[0, at]),
            message((0, -1), src.at[:, y], dst.at[1, at]),
        ]

    def corners_in(src, dst):
        return [
            message(
                side, src.at[Z - 1 if side[0] > 0 else 0, Y - 1 if side[1] > 0 else 0],
                dst.at[i, 0, 0],
            )
            for i, side in enumerate(SIDES[4:])
        ]

    def corners(src, dst):
        return [message(side, src.at[i], dst.at[i]) for i, side in enumerate(SIDES[4:])]

    lane = lax.broadcasted_iota(jnp.int32, (8, 128), 1)
    row = lax.broadcasted_iota(jnp.int32, (8, 128), 0)
    top, bottom = row == 0, row == 7
    first, last = lane == 0, lane == 127

    def block(j):
        return pl.ds(128 * j, 128)

    def layer(buf, z):
        return [[buf[z, pl.ds(8 * t, 8), block(j)] for j in range(C)] for t in range(T)]

    def store(buf, z, t, j, value):
        buf[z, pl.ds(8 * t, 8), block(j)] = value

    def wide_row(buf, *at):
        return [
            jnp.broadcast_to(buf[(*at[:-1], pl.ds(at[-1], 1), block(j))], (8, 128))
            for j in range(C)
        ]

    def shift_x(row_of_tiles, end=None):
        before = [pltpu.roll(c, 1, 1) for c in row_of_tiles]
        after = [pltpu.roll(c, 127, 1) for c in row_of_tiles]
        zero = 0.0
        lo = [
            jnp.where(first, before[j - 1] if j else (zero if end is None else end), before[j])
            for j in range(C)
        ]
        hi = [
            jnp.where(
                last, after[j + 1] if j < C - 1 else (zero if end is None else -end), after[j]
            )
            for j in range(C)
        ]
        return lo, hi

    def shift_y(tiles, lo, hi):
        before = [[pltpu.roll(c, 1, 0) for c in r] for r in tiles]
        after = [[pltpu.roll(c, 7, 0) for c in r] for r in tiles]
        down = [
            [jnp.where(top, before[t - 1][j] if t else lo[j], before[t][j]) for j in range(C)]
            for t in range(T)
        ]
        up = [
            [jnp.where(bottom, after[t + 1][j] if t < T - 1 else hi[j], after[t][j]) for j in range(C)]
            for t in range(T)
        ]
        return down, up

    def sub(a, b):
        if isinstance(a, list):
            return [sub(x, y) for x, y in zip(a, b)]
        return a - b

    def diffs(buf, zc, lo, hi):
        c = layer(buf, zc)
        dz = sub(layer(buf, zc + 1), layer(buf, zc - 1))
        down, up = shift_y(c, lo, hi)
        sides = [shift_x(r) for r in c]
        return c, dz, sub(up, down), [sub(h, l) for l, h in sides]

    def halo_rows(rim, at, z):
        at = () if at is None else (at,)
        if isinstance(z, int):
            return wide_row(rim, 0, *at, z), wide_row(rim, 1, *at, z)
        down = lax.rem(Z - z, 8)
        lo = [pltpu.roll(rim[(0, *at, slice(None), block(j))], down, 0) for j in range(C)]
        hi = [pltpu.roll(rim[(1, *at, slice(None), block(j))], 7 - z, 0) for j in range(C)]
        return lo, hi

    def corner_rows(corner, at, below):
        sz = 1 if below else -1
        lo = SIDES[4:].index((sz, 1))
        hi = SIDES[4:].index((sz, -1))
        return wide_row(corner, lo, at, 0), wide_row(corner, hi, at, 0)

    def ring_diffs(rim, at, edge, edge_at, corner, corner_at, s):
        near = [rim[s, at, :, block(j)] for j in range(C)]
        far = [rim[s, at + 1, :, block(j)] for j in range(C)]
        mine = [edge[s, edge_at, :, block(j)] for j in range(C)]
        sy = 1 if s == 0 else -1
        lo = wide_row(corner, SIDES[4:].index((1, sy)), corner_at, 0)
        hi = wide_row(corner, SIDES[4:].index((-1, sy)), corner_at, 0)
        (dn,), (up,) = ring_shift(near, lo, hi)
        l, h = shift_x(near)
        dy = sub(mine, far) if s == 0 else sub(far, mine)
        return sub(up, dn), dy, sub(h, l)

    def ring_shift(near, lo, hi):
        down = [jnp.where(top, lo[j], pltpu.roll(near[j], 1, 0)) for j in range(C)]
        up = [jnp.where(bottom, hi[j], pltpu.roll(near[j], 7, 0)) for j in range(C)]
        return [down], [up]

    def pack(src, base, deep, dst, at, skip=0):
        for k in range(skip, deep):
            for s, y in ((0, k), (1, Y - 1 - k)):
                total = wide_row(src, base, y)
                for z in range(1, Z):
                    now = wide_row(src, base + z, y)
                    total = [jnp.where(row == z, n, o) for n, o in zip(now, total)]
                for j in range(C):
                    dst[s, at + k, :, block(j)] = total[j]

    def pack_corner(src, dst):
        for i, (sz, sy) in enumerate(SIDES[4:]):
            zc = Z + 1 if sz > 0 else 2
            yc = Y - 1 if sy > 0 else 0
            dst[i, 0] = src[zc, pl.ds(yc, 1), :]

    def ends(tiles):
        return jnp.where(first, tiles[0], jnp.where(last, tiles[C - 1], 0.0))

    def end_basis(d):
        xx = d * d
        r = recip(xx + FLOOR)
        qs = xx * xx * r
        q = qs * r
        a = BASE + RISE * q
        return d, xx, r, qs, q, a, a * (HALF_BASE - FALL * q), TWIST * a * r

    def end_flux(b):
        d, xx, r, qs, q, a, big_a, big_b = b
        return d * (big_a + big_b * xx)

    def end_tangent(b, e):
        d, xx, r, qs, q, a, big_a, big_b = b
        m = d * e
        dq = (4.0 * r * r) * (xx * m - qs * m)
        d_a = (SLOPE_0 + SLOPE_1 * q) * dq
        d_b = r * (TWIST * RISE * dq - (2.0 * TWIST) * a * r * m)
        return (big_a + 3.0 * big_b * xx) * e + d * (d_a + d_b * xx)

    def cross(fx, fy, end):
        out = []
        down, up = shift_y(fy, [0.0] * C, [0.0] * C)
        for t in range(T):
            l, h = shift_x(fx[t], end[t])
            out.append([(h[j] - l[j]) + (up[t][j] - down[t][j]) for j in range(C)])
        return out

    def blank():
        return [[None] * C for _ in range(T)]

    def flux_layer(p, zc, p_rows, d=None, d_rows=None, with_flux=True, ring=None):
        c, dz, dy, dx = diffs(p, zc, *p_rows)
        if d is not None:
            e, ez, ey, ex = diffs(d, zc, *d_rows)
        fx, fy, hx, hy = blank(), blank(), blank(), blank()
        for t in range(T):
            for j in range(C):
                a = (dz[t][j], dy[t][j], dx[t][j])
                b = basis(*a)
                if with_flux:
                    store(jz, zc - 1, t, j, flux_of(a[0], b[0], b))
                    if ring is not None:
                        fy[t][j] = flux_of(a[1], b[1], b)
                        fx[t][j] = flux_of(a[2], b[2], b)
                if d is not None:
                    v = (ez[t][j], ey[t][j], ex[t][j])
                    k = tangent(*a, *v, b)
                    store(gz, zc - 1, t, j, turn(a[0], b[0], v[0], k))
                    if ring is not None:
                        hy[t][j] = turn(a[1], b[1], v[1], k)
                        hx[t][j] = turn(a[2], b[2], v[2], k)
        if ring is None:
            return
        eb = [end_basis(ends(r)) for r in c]
        if with_flux:
            out = cross(fx, fy, [end_flux(b) for b in eb])
            for t in range(T):
                for j in range(C):
                    store(jxy, ring, t, j, out[t][j])
        if d is not None:
            out = cross(hx, hy, [end_tangent(b, ends(r)) for b, r in zip(eb, e)])
            for t in range(T):
                for j in range(C):
                    store(gxy, ring, t, j, out[t][j])

    def flux_ring(p_args, d_args=None, with_flux=True):
        for s in (0, 1):
            dz, dy, dx = ring_diffs(*p_args, s)
            if d_args is not None:
                ez, ey, ex = ring_diffs(*d_args, s)
            for j in range(C):
                b = basis(dz[j], dy[j], dx[j])
                if with_flux:
                    ring_j[s, :, block(j)] = flux_of(dy[j], b[1], b)
                if d_args is not None:
                    k = tangent(dz[j], dy[j], dx[j], ez[j], ey[j], ex[j], b)
                    ring_g[s, :, block(j)] = turn(dy[j], b[1], ey[j], k)

    def divergence(fz, fxy, ring, z):
        lo, hi = halo_rows(ring, None, z)
        out = blank()
        for t in range(T):
            for j in range(C):
                at = (pl.ds(8 * t, 8), block(j))
                total = (fz[(z + 2, *at)] - fz[(z, *at)]) + fxy[(z, *at)]
                if t == 0:
                    total = jnp.where(top, total - lo[j], total)
                if t == T - 1:
                    total = jnp.where(bottom, total + hi[j], total)
                out[t][j] = 0.25 * total
        return out

    def laplacian(buf, zc, lo, hi):
        c, below, above = layer(buf, zc), layer(buf, zc - 1), layer(buf, zc + 1)
        down, up = shift_y(c, lo, hi)
        out = blank()
        for t in range(T):
            l, h = shift_x(c[t])
            for j in range(C):
                total = (below[t][j] + above[t][j]) + (down[t][j] + up[t][j])
                out[t][j] = c[t][j] + TIME_STEP * (total + (l[j] + h[j]) - 6.0 * c[t][j])
        return out

    def reaction(p, u):
        x = DRIVE_SHARP * (MELT_POINT - u)
        m = DRIVE_SCALE / math.pi * arctan(x)
        well = p * (1.0 - p)
        tilt = p - 0.5 + m
        slope = (-DRIVE_SHARP * DRIVE_SCALE / math.pi) * recip(1.0 + x * x)
        return well * tilt, (1.0 - 2.0 * p) * tilt + well, well * slope

    def over(lo, hi, body, unroll=4):
        if hi - lo <= unroll:
            for z in range(lo, hi):
                body(z)
            return

        def some_layers(i, carry):
            for k in range(unroll):
                body(lo + i * unroll + k)
            return carry
        lax.fori_loop(0, (hi - lo) // unroll, some_layers, 0)
        for z in range(hi - (hi - lo) % unroll, hi):
            body(z)

    def inner(body):
        over(1, Z - 1, body, 3)

    def outer(body):
        body(0)
        body(Z - 1)

    def per_tile(body):
        def whole(z):
            for t in range(T):
                for j in range(C):
                    body(z, t, j)
        return whole

    def with_divergence(fz, fxy, ring, body):
        def whole(z):
            div = divergence(fz, fxy, ring, z)
            for t in range(T):
                for j in range(C):
                    body(z, t, j, div[t][j])
        return whole

    def get(buf, z, t, j):
        return buf[z, pl.ds(8 * t, 8), block(j)]

    m_y0, m_p0 = row_in(p_in, 0, ry0, 0), thick_in(p_in, p0)
    m_f0, m_c0 = row_in(p_in, 1, ry0, 1), corners_in(p_in, rc0)
    m_d1, m_y1, m_c1 = thick(d1), along_y(sy1, ry1, 1, 2), corners(sc1, rc1)
    m_ut = thin_in(u_in, u0) + thin_in(ts_in, t1)
    m_ut += row_in(u_in, 0, ry1, 0) + row_in(ts_in, 0, ry1, 3)
    m_y2, m_p1 = along_y(sy2, ry2, 0), thick(p1)
    m_f2, m_c2 = along_y(sy2, ry2, 1), corners(sc2, rc2)
    m_y3, m_d0, m_t0 = along_y(sy3, ry3, 0), thick(d0), thin(t0)
    m_f3, m_c3 = along_y(sy3, ry3, 1, 2), corners(sc3, rc3)

    @pl.when(zi == 0)
    def _():
        for buf in (p0, p1, d1, d0):
            buf[pl.ds(0, 2)] = jnp.zeros((2,) + buf.shape[1:], jnp.float32)
        for buf in (u0, t1, t0):
            buf[0] = jnp.zeros(buf.shape[1:], jnp.float32)

    @pl.when(zi == nz - 1)
    def _():
        for buf in (p0, p1, d1, d0):
            buf[pl.ds(Z + 2, 2)] = jnp.zeros((2,) + buf.shape[1:], jnp.float32)
        for buf in (u0, t1, t0):
            buf[Z + 1] = jnp.zeros(buf.shape[1:], jnp.float32)

    for s, at_end in ((0, yi == 0), (1, yi == ny - 1)):
        @pl.when(at_end)
        def _(s=s):
            for buf in (ry0, ry1, ry2, ry3):
                buf[s] = jnp.zeros(buf.shape[1:], jnp.float32)

    for i, side in enumerate(SIDES[4:]):
        @pl.when(jnp.logical_not(there(opposite(side))))
        def _(i=i):
            for buf in (rc0, rc1, rc2, rc3):
                buf[i] = jnp.zeros(buf.shape[1:], jnp.float32)

    def one(cond):
        return jnp.where(cond, 1, 0)

    near_z = one(zi > 0) + one(zi < nz - 1)
    near_y = one(yi > 0) + one(yi < ny - 1)
    pl.semaphore_wait(barrier, near_z + near_y + near_z * near_y)
    start(m_y0 + m_p0 + m_f0 + m_c0)

    for copy in local[:6]:
        copy.wait()

    @per_tile
    def weight(z, t, j):
        w = get(sb, z, t, j) + LATENT_HEAT * get(t1, z + 1, t, j)
        store(d1, z + 2, t, j, TIME_STEP * get(kb, z, t, j) * w)
    over(0, Z, weight)
    pack(d1, 2, 2, sy1, 1)
    pack_corner(d1, sc1)
    start(m_d1 + m_y1 + m_c1 + m_ut)
    for copy in local[6:]:
        copy.wait()

    @per_tile
    def first_terms(z, t, j):
        a, b, c = reaction(get(p0, z + 2, t, j), get(u0, z + 1, t, j))
        store(r0, z, t, j, a)
        store(rp0, z, t, j, b)
        store(ru0, z, t, j, c)
    over(0, Z, first_terms)

    def flux0(z):
        flux_layer(p0, z + 2, halo_rows(ry0, 0, z), ring=z)
    arrive(m_y0)
    inner(flux0)
    arrive(m_f0 + m_c0)
    flux_ring((ry0, 0, sy0, 0, rc0, 0))
    arrive(m_p0)
    outer(flux0)
    flux_layer(p0, 1, corner_rows(rc0, 0, True))
    flux_layer(p0, Z + 2, corner_rows(rc0, 0, False))

    def advance_cell(z, t, j, div):
        growth = div + get(r0, z, t, j)
        store(gr0, z, t, j, growth)
        gain = TIME_STEP * get(kb, z, t, j) * growth
        store(p1, z + 2, t, j, get(p0, z + 2, t, j) + gain)
    advance = with_divergence(jz, jxy, ring_j, advance_cell)
    over(0, Z, advance)
    pack(p1, 2, 1, sy2, 0)
    start(m_y2 + m_p1)
    pack_corner(p1, sc2)
    start(m_c2)
    pack(p1, 2, 2, sy2, 0, 1)
    start(m_f2)

    arrive(m_ut)

    def second_terms(z):
        new_u = laplacian(u0, z + 1, *halo_rows(ry1, 0, z))
        new_t = laplacian(t1, z + 1, *halo_rows(ry1, 3, z))
        for t in range(T):
            for j in range(C):
                p = get(p1, z + 2, t, j)
                u = new_u[t][j] + LATENT_HEAT * (p - get(p0, z + 2, t, j))
                a, b, c = reaction(p, u)
                store(r1, z, t, j, a)
                store(rp1, z, t, j, b)
                store(ru1, z, t, j, c)
                store(tl1, z, t, j, new_t[t][j])
    over(0, Z, second_terms, 2)

    def adjoint1(z):
        flux_layer(p1, z + 2, halo_rows(ry2, 0, z), d1, halo_rows(ry1, 1, z), ring=z)
    arrive(m_y1 + m_c1 + m_d1 + m_y2)
    inner(adjoint1)
    arrive(m_f2 + m_c2)
    flux_ring((ry2, 0, sy2, 0, rc2, 0), (ry1, 1, sy1, 1, rc1, 0))
    arrive(m_p1)
    outer(adjoint1)
    flux_layer(p1, 1, corner_rows(rc2, 0, True), d1, corner_rows(rc1, 0, True))
    flux_layer(p1, Z + 2, corner_rows(rc2, 0, False), d1, corner_rows(rc1, 0, False))

    def middle_cell(z, t, j, div):
        d = get(d1, z + 2, t, j)
        pb = get(sb, z, t, j) + d * get(rp1, z, t, j) + div
        ub = get(tl1, z, t, j) + d * get(ru1, z, t, j)
        store(pb0, z, t, j, pb)
        store(t0, z + 1, t, j, ub)
        store(d0, z + 2, t, j, TIME_STEP * get(kb, z, t, j) * (pb + LATENT_HEAT * ub))
    middle = with_divergence(gz, gxy, ring_g, middle_cell)
    over(0, Z, middle)
    pack(d0, 2, 1, sy3, 0)
    start(m_y3 + m_d0)
    pack_corner(d0, sc3)
    start(m_c3)
    pack(d0, 2, 2, sy3, 0, 1)
    pack(t0, 1, 1, sy3, 2)
    start(m_f3 + m_t0)

    def mobility_cell(z, t, j, div):
        growth = div + get(r1, z, t, j)
        late = get(sb, z, t, j) + LATENT_HEAT * get(t1, z + 1, t, j)
        early = get(pb0, z, t, j) + LATENT_HEAT * get(t0, z + 1, t, j)
        store(gm_out, z, t, j, TIME_STEP * (late * growth + early * get(gr0, z, t, j)))
    mobility = with_divergence(jz, jxy, ring_j, mobility_cell)
    over(0, Z, mobility)

    def adjoint0(z):
        flux_layer(p0, z + 2, halo_rows(ry0, 0, z), d0, halo_rows(ry3, 0, z), False, ring=z)
    arrive(m_y3)
    inner(adjoint0)
    arrive(m_f3 + m_c3)
    flux_ring((ry0, 0, sy0, 0, rc0, 0), (ry3, 0, sy3, 0, rc3, 0), False)
    arrive(m_d0 + m_t0)
    outer(adjoint0)
    flux_layer(p0, 1, corner_rows(rc0, 0, True), d0, corner_rows(rc3, 0, True), False)
    flux_layer(p0, Z + 2, corner_rows(rc0, 0, False), d0, corner_rows(rc3, 0, False), False)

    def finish(z):
        new_t = laplacian(t0, z + 1, *halo_rows(ry3, 2, z))
        div = divergence(gz, gxy, ring_g, z)
        for t in range(T):
            for j in range(C):
                d = get(d0, z + 2, t, j)
                pb = get(pb0, z, t, j) + d * get(rp0, z, t, j)
                store(sp_out, z, t, j, pb + div[t][j])
                store(st_out, z, t, j, new_t[t][j] + d * get(ru0, z, t, j))
    over(0, Z, finish, 2)
    sent(m_y0 + m_p0 + m_f0 + m_c0 + m_d1 + m_y1 + m_c1 + m_ut)
    sent(m_y2 + m_p1 + m_f2 + m_c2 + m_y3 + m_d0 + m_t0 + m_f3 + m_c3)


def deliver(*refs):
    ins, outs, sem = refs[:3], refs[3:6], refs[6]
    Z = ins[0].shape[0]
    copies = []
    for src, dst in zip(ins, outs):
        for z in range(0, Z, 2):
            part = pl.ds(z, 2)
            copies.append(pltpu.make_async_copy(src.at[part], dst.at[part], sem.at[len(copies)]))
            copies[-1].start()
    for copy in copies:
        copy.wait()


def body(nz, ny, *blocks):
    Z, Y, X = blocks[0].shape

    def buf(*shape):
        return pltpu.VMEM(shape, jnp.float32)

    thick, thin, flat = (Z + 4, Y, X), (Z + 2, Y, X), (Z, Y, X)
    scratch = [buf(*thick)] * 4 + [buf(*thin)] * 3 + [buf(*flat)] * 3
    scratch += [buf(*thin), buf(*flat)] * 2
    scratch += [buf(*flat)] * 9
    scratch += [buf(2, Z, X)] * 2
    scratch += [buf(2, n, Z, X) for n in (2, 2, 4, 4, 2, 2, 3, 3)]
    scratch += [buf(4, 1, 1, X)] * 8
    count = 48
    scratch += [pltpu.SemaphoreType.DMA((count,))] * 2 + [pltpu.SemaphoreType.DMA((12,))]
    hbm = pl.BlockSpec(memory_space=pltpu.HBM)
    vmem = pl.BlockSpec(memory_space=pltpu.VMEM)
    kept = pltpu.VMEM((Z, Y, X), jnp.float32)
    out = jax.ShapeDtypeStruct((Z, Y, X), jnp.float32)
    results = pl.pallas_call(
        functools.partial(kernel, nz, ny),
        out_shape=(kept, kept, kept),
        in_specs=[hbm] * 5,
        out_specs=(vmem, vmem, vmem),
        scratch_shapes=scratch,
        compiler_params=pltpu.CompilerParams(
            collective_id=0, has_side_effects=True, vmem_limit_bytes=62 * 1024 * 1024
        ),
    )(*blocks)
    return pl.pallas_call(
        deliver,
        out_shape=(out, out, out),
        in_specs=[vmem] * 3,
        out_specs=(hbm, hbm, hbm),
        scratch_shapes=[pltpu.SemaphoreType.DMA((3 * (Z // 2),))],
        compiler_params=pltpu.CompilerParams(vmem_limit_bytes=8 * 1024 * 1024),
    )(*results)


def solution(mesh):
    spec = P("gz", "gy", None)
    return jax.shard_map(
        functools.partial(body, mesh.shape["gz"], mesh.shape["gy"]),
        mesh=mesh,
        in_specs=(spec,) * 5,
        out_specs=(spec,) * 3,
        check_vma=False,
    )
```

```python
import functools
import math

import jax
import jax.numpy as jnp
from jax import lax
from jax.experimental import pallas as pl
from jax.experimental.pallas import tpu as pltpu
from jax.sharding import PartitionSpec as P

TIME_STEP = 0.15
ANISOTROPY = 0.05
GRAD_FLOOR = 0.01
LATENT_HEAT = 1.8
DRIVE_SCALE = 0.9
DRIVE_SHARP = 10.0
MELT_POINT = 1.0

BASE = 1.0 - 3.0 * ANISOTROPY
RISE = 4.0 * ANISOTROPY
HALF_BASE = 0.5 * BASE
FALL = 8.0 * ANISOTROPY - 0.5 * RISE
TWIST = 8.0 * ANISOTROPY
SLOPE_0 = RISE * HALF_BASE - FALL * BASE
SLOPE_1 = -2.0 * RISE * FALL
FLOOR = 4.0 * GRAD_FLOOR

ATAN = (
    1.0, -0.3333328366279602, 0.19998230040073395, -0.14261573553085327,
    0.10940198600292206, -0.08372063934803009, 0.05746355652809143,
    -0.030717508867383003, 0.010680719278752804, -0.0017437011701986194,
)

SIDES = ((1, 0), (-1, 0), (0, 1), (0, -1), (1, 1), (1, -1), (-1, 1), (-1, -1))


def recip(x):
    r = pl.reciprocal(x, approx=True)
    return r * (2.0 - x * r)


def arctan(x):
    size = jnp.abs(x)
    big = size > 1.0
    y = jnp.where(big, recip(jnp.maximum(size, 1.0)), size)
    z = y * y
    total = jnp.full_like(z, ATAN[-1])
    for c in ATAN[-2::-1]:
        total = total * z + c
    total = total * y
    total = jnp.where(big, 0.5 * math.pi - total, total)
    return jnp.where(x < 0.0, -total, total)


def basis(dz, dy, dx):
    zz, yy, xx = dz * dz, dy * dy, dx * dx
    s = zz + yy + xx + FLOOR
    r = recip(s)
    qs = (zz * zz + yy * yy + xx * xx) * r
    q = qs * r
    a = BASE + RISE * q
    big_a = a * (HALF_BASE - FALL * q)
    big_b = TWIST * a * r
    return zz, yy, xx, r, qs, q, a, big_a, big_b


def flux_of(d, sq, b):
    return d * (b[7] + b[8] * sq)


def tangent(dz, dy, dx, ez, ey, ex, b):
    zz, yy, xx, r, qs, q, a, big_a, big_b = b
    mz, my, mx = dz * ez, dy * ey, dx * ex
    g = mz + my + mx
    t = zz * mz + yy * my + xx * mx
    dq = (4.0 * r * r) * (t - qs * g)
    d_a = (SLOPE_0 + SLOPE_1 * q) * dq
    d_b = r * (TWIST * RISE * dq - (2.0 * TWIST) * a * r * g)
    return big_a, 3.0 * big_b, d_a, d_b


def turn(d, sq, e, t):
    return (t[0] + t[1] * sq) * e + d * (t[2] + t[3] * sq)


def kernel(
    nz, ny,
    p_in, u_in, k_in, ps_in, ts_in,
    sp_out, st_out, gm_out,
    p0, p1, d1, d0, u0, t1, t0, u1, kb, sb,
    jz, jxy, gz, gxy,
    r0, rp0, ru0, r1, rp1, ru1, tl1, gr0, pb0,
    ring_j, ring_g, held,
    sy0, ry0, sy1, ry1, sy2, ry2, sy3, ry3,
    sc0, rc0, sc1, rc1, sc2, rc2, sc3, rc3,
    ssem, rsem, lsem,
):
    Z, Y, X = p_in.shape
    T, C = Y // 8, X // 128
    zi, yi = lax.axis_index("gz"), lax.axis_index("gy")

    def there(side):
        cond = None
        for step, at, count in ((side[0], zi, nz), (side[1], yi, ny)):
            if step:
                c = at < count - 1 if step > 0 else at > 0
                cond = c if cond is None else jnp.logical_and(cond, c)
        return cond

    def opposite(side):
        return (-side[0], -side[1])

    barrier = pltpu.get_barrier_semaphore()
    for side in SIDES:
        @pl.when(there(side))
        def _(side=side):
            pl.semaphore_signal(
                barrier, inc=1, device_id=(zi + side[0], yi + side[1]),
                device_id_type=pl.DeviceIdType.MESH,
            )

    local = [
        pltpu.make_async_copy(src, dst, lsem.at[i])
        for i, (src, dst) in enumerate(
            [
                (src.at[pl.ds(z, Z // 2)], dst.at[pl.ds(base + z, Z // 2)])
                for src, dst, base in (
                    (ps_in, sb, 0), (ts_in, t1, 1), (k_in, kb, 0), (p_in, p0, 2), (u_in, u0, 1)
                )
                for z in (0, Z // 2)
            ]
            + [(p_in.at[:, 0], sy0.at[0, 0]), (p_in.at[:, Y - 1], sy0.at[1, 0])]
        )
    ]
    for copy in local:
        copy.start()

    slots = iter(range(rsem.shape[0]))

    def message(side, src, dst):
        slot = next(slots)
        copy = pltpu.make_async_remote_copy(
            src_ref=src, dst_ref=dst, send_sem=ssem.at[slot], recv_sem=rsem.at[slot],
            device_id=(zi + side[0], yi + side[1]), device_id_type=pl.DeviceIdType.MESH,
        )
        return side, copy

    def start(messages):
        for side, copy in messages:
            pl.when(there(side))(copy.start)

    def arrive(messages):
        for side, copy in messages:
            pl.when(there(opposite(side)))(copy.wait_recv)

    def sent(messages):
        for side, copy in messages:
            pl.when(there(side))(copy.wait_send)

    def thick(buf):
        return [
            message((1, 0), buf.at[pl.ds(Z, 2)], buf.at[pl.ds(0, 2)]),
            message((-1, 0), buf.at[pl.ds(2, 2)], buf.at[pl.ds(Z + 2, 2)]),
        ]

    def thin(buf):
        return [
            message((1, 0), buf.at[pl.ds(Z, 1)], buf.at[pl.ds(0, 1)]),
            message((-1, 0), buf.at[pl.ds(1, 1)], buf.at[pl.ds(Z + 1, 1)]),
        ]

    def along_y(src, dst, at, deep=1):
        part = pl.ds(at, deep)
        return [
            message((0, 1), src.at[1, part], dst.at[0, part]),
            message((0, -1), src.at[0, part], dst.at[1, part]),
        ]

    def thick_in(src, buf):
        return [
            message((1, 0), src.at[pl.ds(Z - 2, 2)], buf.at[pl.ds(0, 2)]),
            message((-1, 0), src.at[pl.ds(0, 2)], buf.at[pl.ds(Z + 2, 2)]),
        ]

    def thin_in(src, buf):
        return [
            message((1, 0), src.at[pl.ds(Z - 1, 1)], buf.at[pl.ds(0, 1)]),
            message((-1, 0), src.at[pl.ds(0, 1)], buf.at[pl.ds(Z + 1, 1)]),
        ]

    def row_in(src, y, dst, at):
        return [
            message((0, 1), src.at[:, Y - 1 - y], dst.at[0, at]),
            message((0, -1), src.at[:, y], dst.at[1, at]),
        ]

    def corners_in(src, dst):
        return [
            message(
                side, src.at[Z - 1 if side[0] > 0 else 0, Y - 1 if side[1] > 0 else 0],
                dst.at[i, 0, 0],
            )
            for i, side in enumerate(SIDES[4:])
        ]

    def corners(src, dst):
        return [message(side, src.at[i], dst.at[i]) for i, side in enumerate(SIDES[4:])]

    lane = lax.broadcasted_iota(jnp.int32, (8, 128), 1)
    row = lax.broadcasted_iota(jnp.int32, (8, 128), 0)
    top, bottom = row == 0, row == 7
    first, last = lane == 0, lane == 127

    def block(j):
        return pl.ds(128 * j, 128)

    def layer(buf, z):
        return [[buf[z, pl.ds(8 * t, 8), block(j)] for j in range(C)] for t in range(T)]

    def store(buf, z, t, j, value):
        buf[z, pl.ds(8 * t, 8), block(j)] = value

    def wide_row(buf, *at):
        return [
            jnp.broadcast_to(buf[(*at[:-1], pl.ds(at[-1], 1), block(j))], (8, 128))
            for j in range(C)
        ]

    def shift_x(row_of_tiles, end=None):
        before = [pltpu.roll(c, 1, 1) for c in row_of_tiles]
        after = [pltpu.roll(c, 127, 1) for c in row_of_tiles]
        zero = 0.0
        lo = [
            jnp.where(first, before[j - 1] if j else (zero if end is None else end), before[j])
            for j in range(C)
        ]
        hi = [
            jnp.where(
                last, after[j + 1] if j < C - 1 else (zero if end is None else -end), after[j]
            )
            for j in range(C)
        ]
        return lo, hi

    def shift_y(tiles, lo, hi):
        before = [[pltpu.roll(c, 1, 0) for c in r] for r in tiles]
        after = [[pltpu.roll(c, 7, 0) for c in r] for r in tiles]
        down = [
            [jnp.where(top, before[t - 1][j] if t else lo[j], before[t][j]) for j in range(C)]
            for t in range(T)
        ]
        up = [
            [jnp.where(bottom, after[t + 1][j] if t < T - 1 else hi[j], after[t][j]) for j in range(C)]
            for t in range(T)
        ]
        return down, up

    def sub(a, b):
        if isinstance(a, list):
            return [sub(x, y) for x, y in zip(a, b)]
        return a - b

    def diffs(buf, zc, lo, hi):
        c = layer(buf, zc)
        dz = sub(layer(buf, zc + 1), layer(buf, zc - 1))
        down, up = shift_y(c, lo, hi)
        sides = [shift_x(r) for r in c]
        return c, dz, sub(up, down), [sub(h, l) for l, h in sides]

    def halo_rows(rim, at, z):
        at = () if at is None else (at,)
        if isinstance(z, int):
            return wide_row(rim, 0, *at, z), wide_row(rim, 1, *at, z)
        down = lax.rem(Z - z, 8)
        lo = [pltpu.roll(rim[(0, *at, slice(None), block(j))], down, 0) for j in range(C)]
        hi = [pltpu.roll(rim[(1, *at, slice(None), block(j))], 7 - z, 0) for j in range(C)]
        return lo, hi

    def corner_rows(corner, at, below):
        sz = 1 if below else -1
        lo = SIDES[4:].index((sz, 1))
        hi = SIDES[4:].index((sz, -1))
        return wide_row(corner, lo, at, 0), wide_row(corner, hi, at, 0)

    def ring_diffs(rim, at, edge, edge_at, corner, corner_at, s):
        near = [rim[s, at, :, block(j)] for j in range(C)]
        far = [rim[s, at + 1, :, block(j)] for j in range(C)]
        mine = [edge[s, edge_at, :, block(j)] for j in range(C)]
        sy = 1 if s == 0 else -1
        lo = wide_row(corner, SIDES[4:].index((1, sy)), corner_at, 0)
        hi = wide_row(corner, SIDES[4:].index((-1, sy)), corner_at, 0)
        (dn,), (up,) = ring_shift(near, lo, hi)
        l, h = shift_x(near)
        dy = sub(mine, far) if s == 0 else sub(far, mine)
        return sub(up, dn), dy, sub(h, l)

    def ring_shift(near, lo, hi):
        down = [jnp.where(top, lo[j], pltpu.roll(near[j], 1, 0)) for j in range(C)]
        up = [jnp.where(bottom, hi[j], pltpu.roll(near[j], 7, 0)) for j in range(C)]
        return [down], [up]

    def pack(src, base, deep, dst, at, skip=0):
        for k in range(skip, deep):
            for s, y in ((0, k), (1, Y - 1 - k)):
                total = wide_row(src, base, y)
                for z in range(1, Z):
                    now = wide_row(src, base + z, y)
                    total = [jnp.where(row == z, n, o) for n, o in zip(now, total)]
                for j in range(C):
                    dst[s, at + k, :, block(j)] = total[j]

    def pack_corner(src, dst):
        for i, (sz, sy) in enumerate(SIDES[4:]):
            zc = Z + 1 if sz > 0 else 2
            yc = Y - 1 if sy > 0 else 0
            dst[i, 0] = src[zc, pl.ds(yc, 1), :]

    def ends(tiles):
        return jnp.where(first, tiles[0], jnp.where(last, tiles[C - 1], 0.0))

    def end_basis(d):
        xx = d * d
        r = recip(xx + FLOOR)
        qs = xx * xx * r
        q = qs * r
        a = BASE + RISE * q
        return d, xx, r, qs, q, a, a * (HALF_BASE - FALL * q), TWIST * a * r

    def end_flux(b):
        d, xx, r, qs, q, a, big_a, big_b = b
        return d * (big_a + big_b * xx)

    def end_tangent(b, e):
        d, xx, r, qs, q, a, big_a, big_b = b
        m = d * e
        dq = (4.0 * r * r) * (xx * m - qs * m)
        d_a = (SLOPE_0 + SLOPE_1 * q) * dq
        d_b = r * (TWIST * RISE * dq - (2.0 * TWIST) * a * r * m)
        return (big_a + 3.0 * big_b * xx) * e + d * (d_a + d_b * xx)

    def cross(fx, fy, end):
        out = []
        down, up = shift_y(fy, [0.0] * C, [0.0] * C)
        for t in range(T):
            l, h = shift_x(fx[t], end[t])
            out.append([(h[j] - l[j]) + (up[t][j] - down[t][j]) for j in range(C)])
        return out

    def blank():
        return [[None] * C for _ in range(T)]

    def flux_layer(p, zc, p_rows, d=None, d_rows=None, with_flux=True, ring=None):
        c, dz, dy, dx = diffs(p, zc, *p_rows)
        if d is not None:
            e, ez, ey, ex = diffs(d, zc, *d_rows)
        fx, fy, hx, hy = blank(), blank(), blank(), blank()
        for t in range(T):
            for j in range(C):
                a = (dz[t][j], dy[t][j], dx[t][j])
                b = basis(*a)
                if with_flux:
                    store(jz, zc - 1, t, j, flux_of(a[0], b[0], b))
                    if ring is not None:
                        fy[t][j] = flux_of(a[1], b[1], b)
                        fx[t][j] = flux_of(a[2], b[2], b)
                if d is not None:
                    v = (ez[t][j], ey[t][j], ex[t][j])
                    k = tangent(*a, *v, b)
                    store(gz, zc - 1, t, j, turn(a[0], b[0], v[0], k))
                    if ring is not None:
                        hy[t][j] = turn(a[1], b[1], v[1], k)
                        hx[t][j] = turn(a[2], b[2], v[2], k)
        if ring is None:
            return
        eb = [end_basis(ends(r)) for r in c]
        if with_flux:
            out = cross(fx, fy, [end_flux(b) for b in eb])
            for t in range(T):
                for j in range(C):
                    store(jxy, ring, t, j, out[t][j])
        if d is not None:
            out = cross(hx, hy, [end_tangent(b, ends(r)) for b, r in zip(eb, e)])
            for t in range(T):
                for j in range(C):
                    store(gxy, ring, t, j, out[t][j])

    def hold_layer(zc, p_rows):
        _, dz, dy, dx = diffs(p0, zc, *p_rows)
        for t in range(T):
            for j in range(C):
                a = (dz[t][j], dy[t][j], dx[t][j])
                b = basis(*a)
                for i, value in enumerate((*a, b[3], b[4], b[7], 3.0 * b[8])):
                    held[i, zc - 1, pl.ds(8 * t, 8), block(j)] = value

    def held_layer(zc, d_rows, z=None):
        e, ez, ey, ex = diffs(d0, zc, *d_rows)
        hx, hy = blank(), blank()
        for t in range(T):
            for j in range(C):
                dz, dy, dx, r, qs, big_a, big_b3 = (
                    held[i, zc - 1, pl.ds(8 * t, 8), block(j)] for i in range(7)
                )
                v = (ez[t][j], ey[t][j], ex[t][j])
                zz, yy, xx = dz * dz, dy * dy, dx * dx
                q = qs * r
                mz, my, mx = dz * v[0], dy * v[1], dx * v[2]
                g = mz + my + mx
                m = zz * mz + yy * my + xx * mx
                dq = (4.0 * r * r) * (m - qs * g)
                k = (
                    big_a, big_b3, (SLOPE_0 + SLOPE_1 * q) * dq,
                    r * (TWIST * RISE * dq - (2.0 / 3.0) * big_b3 * g),
                )
                store(gz, zc - 1, t, j, turn(dz, zz, v[0], k))
                if z is not None:
                    hy[t][j] = turn(dy, yy, v[1], k)
                    hx[t][j] = turn(dx, xx, v[2], k)
        if z is None:
            return
        c = layer(p0, zc)
        out = cross(hx, hy, [end_tangent(end_basis(ends(a)), ends(b)) for a, b in zip(c, e)])
        for t in range(T):
            for j in range(C):
                store(gxy, z, t, j, out[t][j])

    def flux_ring(p_args, d_args=None, with_flux=True):
        for s in (0, 1):
            dz, dy, dx = ring_diffs(*p_args, s)
            if d_args is not None:
                ez, ey, ex = ring_diffs(*d_args, s)
            for j in range(C):
                b = basis(dz[j], dy[j], dx[j])
                if with_flux:
                    ring_j[s, :, block(j)] = flux_of(dy[j], b[1], b)
                if d_args is not None:
                    k = tangent(dz[j], dy[j], dx[j], ez[j], ey[j], ex[j], b)
                    ring_g[s, :, block(j)] = turn(dy[j], b[1], ey[j], k)

    def divergence(fz, fxy, ring, z):
        lo, hi = halo_rows(ring, None, z)
        out = blank()
        for t in range(T):
            for j in range(C):
                at = (pl.ds(8 * t, 8), block(j))
                total = (fz[(z + 2, *at)] - fz[(z, *at)]) + fxy[(z, *at)]
                if t == 0:
                    total = jnp.where(top, total - lo[j], total)
                if t == T - 1:
                    total = jnp.where(bottom, total + hi[j], total)
                out[t][j] = 0.25 * total
        return out

    def laplacian(buf, zc, lo, hi):
        c, below, above = layer(buf, zc), layer(buf, zc - 1), layer(buf, zc + 1)
        down, up = shift_y(c, lo, hi)
        out = blank()
        for t in range(T):
            l, h = shift_x(c[t])
            for j in range(C):
                total = (below[t][j] + above[t][j]) + (down[t][j] + up[t][j])
                out[t][j] = c[t][j] + TIME_STEP * (total + (l[j] + h[j]) - 6.0 * c[t][j])
        return out

    def reaction(p, u):
        x = DRIVE_SHARP * (MELT_POINT - u)
        m = DRIVE_SCALE / math.pi * arctan(x)
        well = p * (1.0 - p)
        tilt = p - 0.5 + m
        slope = (-DRIVE_SHARP * DRIVE_SCALE / math.pi) * recip(1.0 + x * x)
        return well * tilt, (1.0 - 2.0 * p) * tilt + well, well * slope

    def over(lo, hi, body, unroll=4):
        if hi - lo <= unroll:
            for z in range(lo, hi):
                body(z)
            return

        def some_layers(i, carry):
            for k in range(unroll):
                body(lo + i * unroll + k)
            return carry
        lax.fori_loop(0, (hi - lo) // unroll, some_layers, 0)
        for z in range(hi - (hi - lo) % unroll, hi):
            body(z)

    def inner(body):
        over(1, Z - 1, body, 3)

    def outer(body):
        body(0)
        body(Z - 1)

    def per_tile(body):
        def whole(z):
            for t in range(T):
                for j in range(C):
                    body(z, t, j)
        return whole

    def with_divergence(fz, fxy, ring, body):
        def whole(z):
            div = divergence(fz, fxy, ring, z)
            for t in range(T):
                for j in range(C):
                    body(z, t, j, div[t][j])
        return whole

    def get(buf, z, t, j):
        return buf[z, pl.ds(8 * t, 8), block(j)]

    m_y0, m_p0 = row_in(p_in, 0, ry0, 0), thick_in(p_in, p0)
    m_f0, m_c0 = row_in(p_in, 1, ry0, 1), corners_in(p_in, rc0)
    m_d1, m_y1, m_c1 = thick(d1), along_y(sy1, ry1, 1, 2), corners(sc1, rc1)
    m_ut = thin_in(u_in, u0) + thin_in(ts_in, t1)
    m_ut += row_in(u_in, 0, ry1, 0) + row_in(ts_in, 0, ry1, 3)
    m_y2, m_p1 = along_y(sy2, ry2, 0), thick(p1)
    m_f2, m_c2 = along_y(sy2, ry2, 1), corners(sc2, rc2)
    m_y3, m_d0, m_t0 = along_y(sy3, ry3, 0), thick(d0), thin(t0)
    m_f3, m_c3 = along_y(sy3, ry3, 1, 2), corners(sc3, rc3)

    @pl.when(zi == 0)
    def _():
        for buf in (p0, p1, d1, d0):
            buf[pl.ds(0, 2)] = jnp.zeros((2,) + buf.shape[1:], jnp.float32)
        for buf in (u0, t1, t0):
            buf[0] = jnp.zeros(buf.shape[1:], jnp.float32)

    @pl.when(zi == nz - 1)
    def _():
        for buf in (p0, p1, d1, d0):
            buf[pl.ds(Z + 2, 2)] = jnp.zeros((2,) + buf.shape[1:], jnp.float32)
        for buf in (u0, t1, t0):
            buf[Z + 1] = jnp.zeros(buf.shape[1:], jnp.float32)

    for s, at_end in ((0, yi == 0), (1, yi == ny - 1)):
        @pl.when(at_end)
        def _(s=s):
            for buf in (ry0, ry1, ry2, ry3):
                buf[s] = jnp.zeros(buf.shape[1:], jnp.float32)

    for i, side in enumerate(SIDES[4:]):
        @pl.when(jnp.logical_not(there(opposite(side))))
        def _(i=i):
            for buf in (rc0, rc1, rc2, rc3):
                buf[i] = jnp.zeros(buf.shape[1:], jnp.float32)

    def one(cond):
        return jnp.where(cond, 1, 0)

    near_z = one(zi > 0) + one(zi < nz - 1)
    near_y = one(yi > 0) + one(yi < ny - 1)
    pl.semaphore_wait(barrier, near_z + near_y + near_z * near_y)
    start(m_y0 + m_p0 + m_f0 + m_c0)

    for copy in local[:6]:
        copy.wait()

    @per_tile
    def weight(z, t, j):
        w = get(sb, z, t, j) + LATENT_HEAT * get(t1, z + 1, t, j)
        store(d1, z + 2, t, j, TIME_STEP * get(kb, z, t, j) * w)
    over(0, Z, weight)
    pack(d1, 2, 2, sy1, 1)
    pack_corner(d1, sc1)
    start(m_d1 + m_y1 + m_c1 + m_ut)
    for copy in local[6:]:
        copy.wait()

    @per_tile
    def first_terms(z, t, j):
        a, b, c = reaction(get(p0, z + 2, t, j), get(u0, z + 1, t, j))
        store(r0, z, t, j, a)
        store(rp0, z, t, j, b)
        store(ru0, z, t, j, c)
    over(0, Z, first_terms)

    def flux0(z):
        flux_layer(p0, z + 2, halo_rows(ry0, 0, z), ring=z)
    arrive(m_y0)
    inner(flux0)
    arrive(m_f0 + m_c0)
    flux_ring((ry0, 0, sy0, 0, rc0, 0))
    arrive(m_p0)
    outer(flux0)
    flux_layer(p0, 1, corner_rows(rc0, 0, True))
    flux_layer(p0, Z + 2, corner_rows(rc0, 0, False))

    def advance_cell(z, t, j, div):
        growth = div + get(r0, z, t, j)
        store(gr0, z, t, j, growth)
        gain = TIME_STEP * get(kb, z, t, j) * growth
        store(p1, z + 2, t, j, get(p0, z + 2, t, j) + gain)
    advance = with_divergence(jz, jxy, ring_j, advance_cell)
    over(0, Z, advance)
    pack(p1, 2, 1, sy2, 0)
    start(m_y2 + m_p1)
    pack_corner(p1, sc2)
    start(m_c2)
    pack(p1, 2, 2, sy2, 0, 1)
    start(m_f2)

    arrive(m_ut)

    def second_terms(z):
        new_u = laplacian(u0, z + 1, *halo_rows(ry1, 0, z))
        new_t = laplacian(t1, z + 1, *halo_rows(ry1, 3, z))
        for t in range(T):
            for j in range(C):
                p = get(p1, z + 2, t, j)
                u = new_u[t][j] + LATENT_HEAT * (p - get(p0, z + 2, t, j))
                a, b, c = reaction(p, u)
                store(r1, z, t, j, a)
                store(rp1, z, t, j, b)
                store(ru1, z, t, j, c)
                store(tl1, z, t, j, new_t[t][j])
    over(0, Z, second_terms, 2)

    def adjoint1(z):
        flux_layer(p1, z + 2, halo_rows(ry2, 0, z), d1, halo_rows(ry1, 1, z), ring=z)
    arrive(m_y1 + m_c1 + m_d1 + m_y2)
    inner(adjoint1)
    arrive(m_f2 + m_c2)
    flux_ring((ry2, 0, sy2, 0, rc2, 0), (ry1, 1, sy1, 1, rc1, 0))
    arrive(m_p1)
    outer(adjoint1)
    flux_layer(p1, 1, corner_rows(rc2, 0, True), d1, corner_rows(rc1, 0, True))
    flux_layer(p1, Z + 2, corner_rows(rc2, 0, False), d1, corner_rows(rc1, 0, False))

    def middle_cell(z, t, j, div):
        d = get(d1, z + 2, t, j)
        pb = get(sb, z, t, j) + d * get(rp1, z, t, j) + div
        ub = get(tl1, z, t, j) + d * get(ru1, z, t, j)
        store(pb0, z, t, j, pb)
        store(t0, z + 1, t, j, ub)
        store(d0, z + 2, t, j, TIME_STEP * get(kb, z, t, j) * (pb + LATENT_HEAT * ub))
    middle = with_divergence(gz, gxy, ring_g, middle_cell)
    over(0, Z, middle)
    pack(d0, 2, 1, sy3, 0)
    start(m_y3 + m_d0)
    pack_corner(d0, sc3)
    start(m_c3)
    pack(d0, 2, 2, sy3, 0, 1)
    pack(t0, 1, 1, sy3, 2)
    start(m_f3 + m_t0)

    def mobility_cell(z, t, j, div):
        growth = div + get(r1, z, t, j)
        late = get(sb, z, t, j) + LATENT_HEAT * get(t1, z + 1, t, j)
        early = get(pb0, z, t, j) + LATENT_HEAT * get(t0, z + 1, t, j)
        store(gm_out, z, t, j, TIME_STEP * (late * growth + early * get(gr0, z, t, j)))
    mobility = with_divergence(jz, jxy, ring_j, mobility_cell)
    over(0, Z, mobility)

    def hold(z):
        hold_layer(z + 2, halo_rows(ry0, 0, z))
    over(0, Z, hold, 2)
    hold_layer(1, corner_rows(rc0, 0, True))
    hold_layer(Z + 2, corner_rows(rc0, 0, False))

    def adjoint0(z):
        held_layer(z + 2, halo_rows(ry3, 0, z), z)
    arrive(m_y3)
    inner(adjoint0)
    arrive(m_f3 + m_c3)
    flux_ring((ry0, 0, sy0, 0, rc0, 0), (ry3, 0, sy3, 0, rc3, 0), False)
    arrive(m_d0 + m_t0)
    outer(adjoint0)
    held_layer(1, corner_rows(rc3, 0, True))
    held_layer(Z + 2, corner_rows(rc3, 0, False))

    def finish(z):
        new_t = laplacian(t0, z + 1, *halo_rows(ry3, 2, z))
        div = divergence(gz, gxy, ring_g, z)
        for t in range(T):
            for j in range(C):
                d = get(d0, z + 2, t, j)
                pb = get(pb0, z, t, j) + d * get(rp0, z, t, j)
                store(sp_out, z, t, j, pb + div[t][j])
                store(st_out, z, t, j, new_t[t][j] + d * get(ru0, z, t, j))
    over(0, Z, finish, 2)
    sent(m_y0 + m_p0 + m_f0 + m_c0 + m_d1 + m_y1 + m_c1 + m_ut)
    sent(m_y2 + m_p1 + m_f2 + m_c2 + m_y3 + m_d0 + m_t0 + m_f3 + m_c3)


def deliver(*refs):
    ins, outs, sem = refs[:3], refs[3:6], refs[6]
    Z = ins[0].shape[0]
    copies = []
    for src, dst in zip(ins, outs):
        for z in range(0, Z, 2):
            part = pl.ds(z, 2)
            copies.append(pltpu.make_async_copy(src.at[part], dst.at[part], sem.at[len(copies)]))
            copies[-1].start()
    for copy in copies:
        copy.wait()


def body(nz, ny, *blocks):
    Z, Y, X = blocks[0].shape

    def buf(*shape):
        return pltpu.VMEM(shape, jnp.float32)

    thick, thin, flat = (Z + 4, Y, X), (Z + 2, Y, X), (Z, Y, X)
    scratch = [buf(*thick)] * 4 + [buf(*thin)] * 3 + [buf(*flat)] * 3
    scratch += [buf(*thin), buf(*flat)] * 2
    scratch += [buf(*flat)] * 9
    scratch += [buf(2, Z, X)] * 2 + [buf(7, *thin)]
    scratch += [buf(2, n, Z, X) for n in (2, 2, 4, 4, 2, 2, 3, 3)]
    scratch += [buf(4, 1, 1, X)] * 8
    count = 48
    scratch += [pltpu.SemaphoreType.DMA((count,))] * 2 + [pltpu.SemaphoreType.DMA((12,))]
    hbm = pl.BlockSpec(memory_space=pltpu.HBM)
    vmem = pl.BlockSpec(memory_space=pltpu.VMEM)
    kept = pltpu.VMEM((Z, Y, X), jnp.float32)
    out = jax.ShapeDtypeStruct((Z, Y, X), jnp.float32)
    results = pl.pallas_call(
        functools.partial(kernel, nz, ny),
        out_shape=(kept, kept, kept),
        in_specs=[hbm] * 5,
        out_specs=(vmem, vmem, vmem),
        scratch_shapes=scratch,
        compiler_params=pltpu.CompilerParams(
            collective_id=0, has_side_effects=True, vmem_limit_bytes=62 * 1024 * 1024
        ),
    )(*blocks)
    return pl.pallas_call(
        deliver,
        out_shape=(out, out, out),
        in_specs=[vmem] * 3,
        out_specs=(hbm, hbm, hbm),
        scratch_shapes=[pltpu.SemaphoreType.DMA((3 * (Z // 2),))],
        compiler_params=pltpu.CompilerParams(vmem_limit_bytes=8 * 1024 * 1024),
    )(*results)


def solution(mesh):
    spec = P("gz", "gy", None)
    return jax.shard_map(
        functools.partial(body, mesh.shape["gz"], mesh.shape["gy"]),
        mesh=mesh,
        in_specs=(spec,) * 5,
        out_specs=(spec,) * 3,
        check_vma=False,
    )
```
